32 devices in a mesh: dp: 32 (over z, y, x, core).
Axes of the slice: x: 2, y: 2, z: 4, core: 2. Of those that a mesh axis runs over, the one named last changes fastest.
Arguments:
- tokens: bfloat16 [65536, 768], P('dp'), may hold values from -6 to 6
- norm_gain: bfloat16 [768], P('dp'), may hold values from 0.099609375 to 1.8984375
- norm_shift: bfloat16 [768], P('dp'), may hold values from -1.75 to 1.75
- query_weight: bfloat16 [768, 768], P('dp'), may hold values from -0.21875 to 0.21875
- query_bias: bfloat16 [768], P('dp'), may hold values from -1.75 to 1.75
- key_weight: bfloat16 [768, 768], P('dp'), may hold values from -0.21875 to 0.21875
- value_weight: bfloat16 [768, 768], P('dp'), may hold values from -0.21875 to 0.21875
- value_bias: bfloat16 [768], P('dp'), may hold values from -1.75 to 1.75
- output_weight: bfloat16 [768, 768], P('dp'), may hold values from -1.25 to 1.25
- output_bias: bfloat16 [768], P('dp'), may hold values from -1.75 to 1.75
- second_gain: bfloat16 [768], P('dp'), may hold values from 0.099609375 to 1.8984375
- second_shift: bfloat16 [768], P('dp'), may hold values from -1.75 to 1.75
- up_weight: bfloat16 [768, 3072], P('dp'), may hold values from -0.21875 to 0.21875
- up_bias: bfloat16 [3072], P('dp'), may hold values from -3 to 3
- down_weight: bfloat16 [3072, 768], P('dp'), may hold values from -0.109375 to 0.109375
- down_bias: bfloat16 [768], P('dp'), may hold values from -1.75 to 1.75
- cotangent: bfloat16 [65536, 768], P('dp'), may hold values from -12 to 12
Outputs:
- mixed: bfloat16 [65536, 768], P('dp')
- input_grad: float32 [65536, 768], P('dp')
- grad_norm_gain: float32 [768], P('dp')
- grad_norm_shift: float32 [768], P('dp')
- grad_query_weight: float32 [768, 768], P('dp')
- grad_query_bias: float32 [768], P('dp')
- grad_key_weight: float32 [768, 768], P('dp')
- grad_value_weight: float32 [768, 768], P('dp')
- grad_value_bias: float32 [768], P('dp')
- grad_output_weight: float32 [768, 768], P('dp')
- grad_output_bias: float32 [768], P('dp')
- grad_second_gain: float32 [768], P('dp')
- grad_second_shift: float32 [768], P('dp')
- grad_up_weight: float32 [768, 3072], P('dp')
- grad_up_bias: float32 [3072], P('dp')
- grad_down_weight: float32 [3072, 768], P('dp')
- grad_down_bias: float32 [768], P('dp')
The draws below stay inside these ranges and needn't reach their ends.
All inputs are finite; a program needn't handle non-finite values.
Results may differ from the reference program's by a relative error of at most 0.011.
Values may be sent and summed in bfloat16 or wider, within the bound.
No kernel may reach another device: no remote copies, remote signals or barrier semaphores. Data moves between devices by JAX's collectives and lax.ppermute only.
A program may use at most 384 MiB of HBM per device.

```python
import math
import jax
import jax.numpy as jnp
from jax import lax

D = 768
H = 12
HD = 64
FF = 3072
SEQ = 1024
TOKENS = 65536


def spiked(values, key, source, target, shards_of, factor):
    def block_of(axis_at):
        return (jnp.arange(values.shape[axis_at]) // (values.shape[axis_at] // shards_of)).reshape((-1,) + (1,) * (values.ndim - 1 - axis_at))

    first = jax.random.permutation(key, shards_of)[block_of(target)]
    other_side = (block_of(target) + shards_of // 2) % shards_of
    return jnp.where((block_of(source) == first) | (block_of(source) == other_side), factor * values, values)


def block_scale(rng, dims, pieces, least, high):
    factor_of, own = 1.0, jax.random.fold_in(rng, 6)
    for dim, parts in pieces:
        steps = jnp.exp(jax.random.uniform(jax.random.fold_in(own, dim), (parts,), jnp.float32, least / len(pieces), high / len(pieces)))
        factor_of = factor_of * jnp.repeat(steps, dims[dim] // parts).reshape([-1 if axis == dim else 1 for axis in range(len(dims))])
    return factor_of


def gaussian(rng, dims, width, limit, pieces=(), held_as=jnp.bfloat16):
    factor_of = block_scale(rng, dims, pieces, -0.22, 0.18) if pieces else 1.0
    entries = jax.random.normal(rng, dims, jnp.float32) * width * factor_of
    return jnp.minimum(jnp.maximum(entries, -limit), limit).astype(held_as)


def bell_draw_with(own_key, shape, deviation, most, split, heavy, held_as=jnp.bfloat16):
    values = deviation * jax.random.normal(own_key, shape, jnp.float32)
    if split:
        values = values * block_scale(own_key, shape, split, -0.22, 0.18)
    return jnp.clip(spiked(values, jax.random.fold_in(own_key, 3), *heavy), -most, most).astype(held_as)


def setup_inputs(seed: int = 0) -> dict:
    splits = jax.random.split(jax.random.key(seed), 18)
    tokens = gaussian(splits[0], (TOKENS, D), 1.0, 6.0, ((0, 32),))
    norm_gain = jnp.clip(1.0 + 0.18 * jax.random.normal(splits[1], (D,), jnp.float32), 0.099609375, 1.8984375).astype(jnp.bfloat16)
    norm_shift = gaussian(splits[2], (D,), 0.3, 1.75, ((0, 32),))
    query_weight = gaussian(splits[3], (D, D), D ** -0.5, 0.21875, ((0, 32),))
    query_bias = gaussian(splits[4], (D,), 0.3, 1.75, ((0, 32),))
    key_weight = gaussian(splits[5], (D, D), D ** -0.5, 0.21875, ((0, 32),))
    value_weight = gaussian(splits[6], (D, D), D ** -0.5, 0.21875, ((0, 32),))
    value_bias = gaussian(splits[7], (D,), 0.3, 1.75, ((0, 32),))
    output_weight = gaussian(splits[8], (D, D), (D // 32) ** -0.5, 1.25, ((0, 32),))
    output_bias = gaussian(splits[9], (D,), 0.3, 1.75, ((0, 32),))
    second_gain = jnp.clip(1.0 + 0.18 * jax.random.normal(splits[10], (D,), jnp.float32), 0.099609375, 1.8984375).astype(jnp.bfloat16)
    second_shift = gaussian(splits[11], (D,), 0.3, 1.75, ((0, 32),))
    up_weight = gaussian(splits[12], (D, FF), D ** -0.5, 0.21875, ((0, 32),))
    up_bias = gaussian(splits[13], (FF,), 0.5, 3.0, ((0, 32),))
    down_weight = gaussian(splits[14], (FF, D), FF ** -0.5, 0.109375, ((0, 32),))
    down_bias = gaussian(splits[15], (D,), 0.3, 1.75, ((0, 32),))
    cotangent = bell_draw_with(splits[16], (TOKENS, D), 1.0, 12.0, ((0, 32),), (0, 1, 32, 2.75))
    return dict(tokens=tokens, norm_gain=norm_gain, norm_shift=norm_shift, query_weight=query_weight, query_bias=query_bias, key_weight=key_weight, value_weight=value_weight, value_bias=value_bias, output_weight=output_weight, output_bias=output_bias, second_gain=second_gain, second_shift=second_shift, up_weight=up_weight, up_bias=up_bias, down_weight=down_weight, down_bias=down_bias, cotangent=cotangent)


epsilon = 1e-05
highest = lax.Precision.HIGHEST

@jax.custom_vjp
def low(v):
    return lax.optimization_barrier(v.astype(jnp.bfloat16)).astype(jnp.float32)

@jax.custom_vjp
def low_back(v):
    return v

def low_keep(v):
    return (low(v), None)

def low_pass(kept, grad):
    return (grad,)

def back_keep(v):
    return (v, None)

def back_low(kept, grad):
    return (low(grad),)
low.defvjp(low_keep, low_pass)
low_back.defvjp(back_keep, back_low)

def layer_norm(values, gain, shift):
    center = values - lax.optimization_barrier(jnp.mean(values, axis=-1, keepdims=True))
    spread = lax.optimization_barrier(jnp.mean(center * center, axis=-1, keepdims=True))
    return center * lax.rsqrt(spread + epsilon) * gain + shift

def matmul(left, right):
    return jnp.dot(left, right, precision=highest)

def attend_sequence(queries, keys_all, values_all):
    block_rows = min(512, SEQ)
    scaling = HD ** (-0.5)
    query_blocks = queries.reshape(SEQ // block_rows, block_rows, H, HD)
    starts = jnp.arange(SEQ // block_rows, dtype=jnp.int32) * block_rows

    @jax.checkpoint
    def one_block(pair):
        query_part, row_start = pair
        scores = jnp.einsum('qhd,khd->hqk', query_part, keys_all, precision=highest) * scaling
        scores = low_back(scores)
        rows_idx = row_start + jnp.arange(block_rows, dtype=jnp.int32)
        cols_idx = jnp.arange(SEQ, dtype=jnp.int32)
        allowed = cols_idx[None, :] <= rows_idx[:, None]
        scores = jnp.where(allowed[None], scores, -jnp.inf)
        probs = low(jax.nn.softmax(scores, axis=-1))
        return jnp.einsum('hqk,khd->qhd', probs, values_all, precision=highest)
    outputs = lax.map(one_block, (query_blocks, starts))
    return outputs.reshape(SEQ, H * HD)

def block_forward(inputs, params):
    norm_gain, norm_shift, query_weight, query_bias, key_weight, value_weight, value_bias, output_weight, output_bias, second_gain, second_shift, up_weight, up_bias, down_weight, down_bias = params
    normed = low(layer_norm(inputs, norm_gain, norm_shift))
    queries = low(low_back(matmul(normed, query_weight) + query_bias))
    keys_low = low(low_back(matmul(normed, key_weight)))
    values_low = low(low_back(matmul(normed, value_weight) + value_bias))
    count = inputs.shape[0] // SEQ
    shape = (count, SEQ, H, HD)
    attended = jax.vmap(attend_sequence)(queries.reshape(shape), keys_low.reshape(shape), values_low.reshape(shape))
    attn_low = low(low_back(attended.reshape(count * SEQ, D)))
    residual = inputs + low_back(matmul(attn_low, output_weight) + output_bias)
    second = low(layer_norm(residual, second_gain, second_shift))
    hidden = low_back(matmul(second, up_weight) + up_bias)
    active = low(jax.nn.gelu(hidden, approximate=True))
    return residual + matmul(active, down_weight) + down_bias

def reference(tokens, norm_gain, norm_shift, query_weight, query_bias, key_weight, value_weight, value_bias, output_weight, output_bias, second_gain, second_shift, up_weight, up_bias, down_weight, down_bias, cotangent):
    params = tuple((p.astype(jnp.float32) for p in (norm_gain, norm_shift, query_weight, query_bias, key_weight, value_weight, value_bias, output_weight, output_bias, second_gain, second_shift, up_weight, up_bias, down_weight, down_bias)))
    count = tokens.shape[0] // SEQ
    group = math.gcd(count, max(1, 4096 // SEQ))
    inputs_all = tokens.astype(jnp.float32).reshape(count // group, group * SEQ, D)
    cot_all = cotangent.astype(jnp.float32).reshape(count // group, group * SEQ, D)

    def step(total, pair):
        input_part, cot_part = pair
        result, pull = jax.vjp(block_forward, input_part, params)
        grad_input, grad_params = pull(cot_part)
        total = jax.tree.map(jnp.add, total, grad_params)
        return (total, (result.astype(jnp.bfloat16), grad_input))
    zeros = jax.tree.map(jnp.zeros_like, params)
    grads, (results, input_grads) = lax.scan(step, zeros, (inputs_all, cot_all))
    mixed = results.reshape(count * SEQ, D)
    input_grad = input_grads.reshape(count * SEQ, D)
    return (mixed, input_grad, grads[0], grads[1], grads[2], grads[3], grads[4], grads[5], grads[6], grads[7], grads[8], grads[9], grads[10], grads[11], grads[12], grads[13], grads[14])
```

```python
import functools

import jax
import jax.numpy as jnp
from jax import lax
from jax.experimental import pallas as pl
from jax.experimental.pallas import tpu as pltpu
from jax.sharding import PartitionSpec as P

HD = 64
SEQ = 1024
LANES = 128
QUERY_BLOCK = 256
F32 = jnp.float32
BF16 = jnp.bfloat16
EPSILON = 1e-05
GELU_SCALE = 0.7978845608028654
GELU_CUBIC = 0.044715


def dot_nn(left, right):
    return lax.dot_general(left, right, (((1,), (0,)), ((), ())), preferred_element_type=F32)


def dot_nt(left, right):
    return lax.dot_general(left, right, (((1,), (1,)), ((), ())), preferred_element_type=F32)


def dot_tn(left, right):
    return lax.dot_general(left, right, (((0,), (0,)), ((), ())), preferred_element_type=F32)


def normalise(values):
    center = values - jnp.mean(values, axis=-1, keepdims=True)
    rstd = lax.rsqrt(jnp.mean(center * center, axis=-1, keepdims=True) + EPSILON)
    return center * rstd, rstd


def whole(shape):
    return pl.BlockSpec(shape, lambda *_: (0,) * len(shape), pipeline_mode=pl.Buffered(1))


def rows(block, width):
    return pl.BlockSpec((block, width), lambda i: (i, 0))


def project_kernel(x_ref, vec_ref, wq_ref, wk_ref, wv_ref, h_ref, q_ref, k_ref, v_ref):
    normed, _ = normalise(x_ref[...].astype(F32))
    h = (normed * vec_ref[0:1, :] + vec_ref[1:2, :]).astype(BF16)
    h_ref[...] = h
    q = (dot_nn(h, wq_ref[...]) + vec_ref[2:3, :]).astype(BF16)
    q_ref[...] = (q.astype(F32) * HD**-0.5).astype(BF16)
    k_ref[...] = dot_nn(h, wk_ref[...]).astype(BF16)
    v_ref[...] = (dot_nn(h, wv_ref[...]) + vec_ref[3:4, :]).astype(BF16)


def project(tokens, vecs, wq, wk, wv):
    count, width = tokens.shape
    block = 512
    out = jax.ShapeDtypeStruct((count, width), BF16)
    return pl.pallas_call(
        project_kernel,
        grid=(count // block,),
        in_specs=[rows(block, width), whole(vecs.shape)] + [whole((width, width))] * 3,
        out_specs=[rows(block, width)] * 4,
        out_shape=[out] * 4,
        compiler_params=pltpu.CompilerParams(vmem_limit_bytes=48 * 2**20),
        cost_estimate=pl.CostEstimate(
            flops=6 * count * width * width,
            bytes_accessed=10 * count * width + 6 * width * width,
            transcendentals=0,
        ),
        name="project",
    )(tokens, vecs, wq, wk, wv)


def head_only(values, head):
    lane = lax.broadcasted_iota(jnp.int32, values.shape, 1)
    keep = (lane < HD) if head == 0 else (lane >= HD)
    return jnp.where(keep, values, jnp.zeros_like(values))


def causal_t(scores_t):
    key = lax.broadcasted_iota(jnp.int32, scores_t.shape, 0)
    query = lax.broadcasted_iota(jnp.int32, scores_t.shape, 1)
    return key <= query


def attend_kernel(q_ref, k_ref, v_ref, o_ref, lse_ref, out_t):
    seq_len = q_ref.shape[0]
    k = k_ref[...]
    v_t = v_ref[...].astype(F32).T.astype(BF16)
    for head in range(2):
        q = head_only(q_ref[...], head)
        v_head = v_t[head * HD : (head + 1) * HD, :]
        for start in range(0, seq_len, QUERY_BLOCK):
            end = start + QUERY_BLOCK
            q_part = q[start:end]
            diag = dot_nt(k[start:end], q_part)
            diag = jnp.where(causal_t(diag), diag, -jnp.inf)
            peak = jnp.max(diag, axis=0, keepdims=True)
            if start:
                full = dot_nt(k[:start], q_part)
                peak = jnp.maximum(peak, jnp.max(full, axis=0, keepdims=True))
            p_diag = jnp.exp(diag - peak)
            total = jnp.sum(p_diag, axis=0, keepdims=True)
            mixed = dot_nn(v_head[:, start:end], p_diag.astype(BF16))
            if start:
                p_full = jnp.exp(full - peak)
                total = total + jnp.sum(p_full, axis=0, keepdims=True)
                mixed = mixed + dot_nn(v_head[:, :start], p_full.astype(BF16))
            out_t[head * HD : (head + 1) * HD, start:end] = mixed * (1.0 / total)
            lse_ref[0, 0, head : head + 1, start:end] = peak + jnp.log(total)
    o_ref[...] = out_t[...].T.astype(BF16)


def attend(q, k, v):
    count, width = q.shape
    seqs, pairs = count // SEQ, width // LANES
    block = pl.BlockSpec((SEQ, LANES), lambda s, p: (s, p))
    return pl.pallas_call(
        attend_kernel,
        grid=(seqs, pairs),
        in_specs=[block] * 3,
        out_specs=[block, pl.BlockSpec((1, 1, 2, SEQ), lambda s, p: (s, p, 0, 0))],
        out_shape=[
            jax.ShapeDtypeStruct((count, width), BF16),
            jax.ShapeDtypeStruct((seqs, pairs, 2, SEQ), F32),
        ],
        scratch_shapes=[pltpu.VMEM((LANES, SEQ), F32)],
        compiler_params=pltpu.CompilerParams(vmem_limit_bytes=48 * 2**20),
        cost_estimate=pl.CostEstimate(
            flops=4 * count * SEQ * width,
            bytes_accessed=8 * count * width,
            transcendentals=count * SEQ * width // HD,
        ),
        name="attend",
    )(q, k, v)


def attend_back_kernel(
    q_ref, k_ref, v_ref, do_ref, lse_ref, dq_ref, dk_ref, dv_ref, sums_ref, dq_t, dk_acc, dv_acc
):
    seq_len = q_ref.shape[0]
    k = k_ref[...]
    v = v_ref[...]
    k_t = k.astype(F32).T.astype(BF16)
    dk_acc[...] = jnp.zeros_like(dk_acc)
    dv_acc[...] = jnp.zeros_like(dv_acc)
    for head in range(2):
        q = head_only(q_ref[...], head)
        do = head_only(do_ref[...], head)
        k_head = k_t[head * HD : (head + 1) * HD, :]
        for start in range(0, seq_len, QUERY_BLOCK):
            end = start + QUERY_BLOCK
            q_part = q[start:end]
            do_part = do[start:end]
            lse = lse_ref[0, 0, head : head + 1, start:end]
            scores = dot_nt(k[start:end], q_part)
            p_diag = jnp.exp(jnp.where(causal_t(scores), scores, -jnp.inf) - lse)
            dp_diag = dot_nt(v[start:end], do_part)
            inner = jnp.sum(p_diag * dp_diag, axis=0, keepdims=True)
            if start:
                p_full = jnp.exp(dot_nt(k[:start], q_part) - lse)
                dp_full = dot_nt(v[:start], do_part)
                inner = inner + jnp.sum(p_full * dp_full, axis=0, keepdims=True)
                ds_full = (p_full * (dp_full - inner)).astype(BF16)
                dv_acc[:start, :] += dot_nn(p_full.astype(BF16), do_part)
                dk_acc[:start, :] += dot_nn(ds_full, q_part)
            ds_diag = (p_diag * (dp_diag - inner)).astype(BF16)
            dv_acc[start:end, :] += dot_nn(p_diag.astype(BF16), do_part)
            dk_acc[start:end, :] += dot_nn(ds_diag, q_part)
            dq = dot_nn(k_head[:, start:end], ds_diag)
            if start:
                dq = dq + dot_nn(k_head[:, :start], ds_full)
            dq_t[head * HD : (head + 1) * HD, start:end] = dq
    dq = (dq_t[...].T * HD**-0.5).astype(BF16)
    dv = dv_acc[...].astype(BF16)
    dq_ref[...] = dq
    dk_ref[...] = dk_acc[...].astype(BF16)
    dv_ref[...] = dv
    sums_ref[0, 0:1, :] = jnp.sum(dq.astype(F32), axis=0, keepdims=True)
    sums_ref[0, 1:2, :] = jnp.sum(dv.astype(F32), axis=0, keepdims=True)


def attend_back(q, k, v, d_attn, lse):
    count, width = q.shape
    seqs, pairs = count // SEQ, width // LANES
    block = pl.BlockSpec((SEQ, LANES), lambda s, p: (s, p))
    out = jax.ShapeDtypeStruct((count, width), BF16)
    return pl.pallas_call(
        attend_back_kernel,
        grid=(seqs, pairs),
        in_specs=[block] * 4 + [pl.BlockSpec((1, 1, 2, SEQ), lambda s, p: (s, p, 0, 0))],
        out_specs=[block] * 3 + [pl.BlockSpec((1, 2, LANES), lambda s, p: (s, 0, p))],
        out_shape=[out] * 3 + [jax.ShapeDtypeStruct((seqs, 2, width), F32)],
        scratch_shapes=[
            pltpu.VMEM((LANES, SEQ), F32),
            pltpu.VMEM((SEQ, LANES), F32),
            pltpu.VMEM((SEQ, LANES), F32),
        ],
        compiler_params=pltpu.CompilerParams(vmem_limit_bytes=48 * 2**20),
        cost_estimate=pl.CostEstimate(
            flops=10 * count * SEQ * width,
            bytes_accessed=14 * count * width,
            transcendentals=count * SEQ * width // HD,
        ),
        name="attend_back",
    )(q, k, v, d_attn, lse)


def feed_kernel(
    x_ref, a_ref, dy_ref, vec_ref, ub_ref, wo_hbm, wu_hbm, wd_hbm,
    mixed_ref, dr_ref, da_ref, gvec_ref, gub_ref, go_hbm, gu_hbm, gd_hbm,
    wo, wu, wd, acc_o, acc_u, acc_d, sems,
):
    step = pl.program_id(0)
    width = x_ref.shape[1]
    pieces = ((wo_hbm, wo, acc_o, go_hbm), (wu_hbm, wu, acc_u, gu_hbm), (wd_hbm, wd, acc_d, gd_hbm))

    @pl.when(step == 0)
    def _():
        for place, (source, held, _, _) in enumerate(pieces):
            pltpu.make_async_copy(source, held, sems.at[place]).start()
        for _, _, total, _ in pieces:
            total[...] = jnp.zeros_like(total)
        gvec_ref[...] = jnp.zeros_like(gvec_ref)
        gub_ref[...] = jnp.zeros_like(gub_ref)
        for place, (source, held, _, _) in enumerate(pieces):
            pltpu.make_async_copy(source, held, sems.at[place]).wait()

    attn = a_ref[...]
    dy = dy_ref[...]
    dy_wide = dy.astype(F32)
    resid = x_ref[...].astype(F32) + dot_nn(attn, wo[...]) + vec_ref[4:5, :]
    normed, rstd = normalise(resid)
    gain = vec_ref[5:6, :]
    h2 = (normed * gain + vec_ref[6:7, :]).astype(BF16)

    def chunk(index, carry):
        mixed, dh2 = carry
        cols = pl.ds(pl.multiple_of(index * width, width), width)
        u = dot_nn(h2, wu[cols, :]) + ub_ref[:, cols]
        d_act = dot_nt(dy, wd[cols, :])
        square = u * u
        tanh = jnp.tanh(GELU_SCALE * u * (1.0 + GELU_CUBIC * square))
        half = 0.5 + 0.5 * tanh
        act = (u * half).astype(BF16)
        slope = half + u * (0.5 - 0.5 * tanh * tanh) * (
            GELU_SCALE * (1.0 + 3.0 * GELU_CUBIC * square)
        )
        du = (d_act * slope).astype(BF16)
        gub_ref[:, cols] += jnp.sum(du.astype(F32), axis=0, keepdims=True)
        acc_d[cols, :] += dot_tn(act, dy)
        acc_u[cols, :] += dot_tn(h2, du)
        return (mixed + dot_nn(act, wd[cols, :]), dh2 + dot_nt(du, wu[cols, :]))

    mixed, dh2 = lax.fori_loop(
        0, wu.shape[0] // width, chunk, (resid + vec_ref[7:8, :], jnp.zeros_like(resid))
    )
    mixed_ref[...] = mixed.astype(BF16)
    g = dh2 * gain
    dr = dy_wide + rstd * (
        g
        - jnp.mean(g, axis=-1, keepdims=True)
        - normed * jnp.mean(g * normed, axis=-1, keepdims=True)
    )
    dr_ref[...] = dr
    da = dr.astype(BF16)
    da_ref[...] = dot_nt(da, wo[...]).astype(BF16)
    acc_o[...] += dot_tn(attn, da)
    gvec_ref[0:1, :] += jnp.sum(da.astype(F32), axis=0, keepdims=True)
    gvec_ref[1:2, :] += jnp.sum(dh2 * normed, axis=0, keepdims=True)
    gvec_ref[2:3, :] += jnp.sum(dh2, axis=0, keepdims=True)
    gvec_ref[3:4, :] += jnp.sum(dy_wide, axis=0, keepdims=True)

    @pl.when(step == pl.num_programs(0) - 1)
    def _():
        for place, (_, held, total, out) in enumerate(pieces):
            held[...] = total[...].astype(BF16)
            pltpu.make_async_copy(held, out, sems.at[place]).start()
        for place, (_, held, _, out) in enumerate(pieces):
            pltpu.make_async_copy(held, out, sems.at[place]).wait()


def feed(tokens, attn, cotangent, vecs, up_bias, wo, wu, wd):
    count, width = tokens.shape
    block = 512
    any_spec = pl.BlockSpec(memory_space=pl.ANY)
    weights = (wo, wu, wd)
    return pl.pallas_call(
        feed_kernel,
        grid=(count // block,),
        in_specs=[rows(block, width)] * 3 + [whole(vecs.shape), whole(up_bias.shape)] + [any_spec] * 3,
        out_specs=[rows(block, width)] * 3 + [whole((4, width)), whole(up_bias.shape)] + [any_spec] * 3,
        out_shape=[
            jax.ShapeDtypeStruct((count, width), BF16),
            jax.ShapeDtypeStruct((count, width), F32),
            jax.ShapeDtypeStruct((count, width), BF16),
            jax.ShapeDtypeStruct((4, width), F32),
            jax.ShapeDtypeStruct(up_bias.shape, F32),
        ] + [jax.ShapeDtypeStruct(w.shape, BF16) for w in weights],
        scratch_shapes=[pltpu.VMEM(w.shape, BF16) for w in weights]
        + [pltpu.VMEM(w.shape, F32) for w in weights]
        + [pltpu.SemaphoreType.DMA((3,))],
        compiler_params=pltpu.CompilerParams(vmem_limit_bytes=60 * 2**20),
        cost_estimate=pl.CostEstimate(
            flops=6 * count * sum(w.size for w in weights),
            bytes_accessed=14 * count * width + 4 * sum(w.size for w in weights),
            transcendentals=count * up_bias.size,
        ),
        name="feed",
    )(tokens, attn, cotangent, vecs, up_bias, wo, wu, wd)


def input_grad_kernel(
    x_ref, dr_ref, dq_ref, dk_ref, dv_ref, vec_ref, wq_ref, wk_ref, wv_ref, ig_ref, sums_ref
):
    @pl.when(pl.program_id(0) == 0)
    def _():
        sums_ref[...] = jnp.zeros_like(sums_ref)

    normed, rstd = normalise(x_ref[...].astype(F32))
    dh = (
        dot_nt(dq_ref[...], wq_ref[...])
        + dot_nt(dk_ref[...], wk_ref[...])
        + dot_nt(dv_ref[...], wv_ref[...])
    )
    g = dh * vec_ref[0:1, :]
    ig_ref[...] = dr_ref[...] + rstd * (
        g
        - jnp.mean(g, axis=-1, keepdims=True)
        - normed * jnp.mean(g * normed, axis=-1, keepdims=True)
    )
    sums_ref[0:1, :] += jnp.sum(dh * normed, axis=0, keepdims=True)
    sums_ref[1:2, :] += jnp.sum(dh, axis=0, keepdims=True)


def input_gradient(tokens, dr, dq, dk, dv, vecs, wq, wk, wv):
    count, width = tokens.shape
    block = 512
    return pl.pallas_call(
        input_grad_kernel,
        grid=(count // block,),
        in_specs=[rows(block, width)] * 5 + [whole(vecs.shape)] + [whole((width, width))] * 3,
        out_specs=[rows(block, width), whole((2, width))],
        out_shape=[
            jax.ShapeDtypeStruct((count, width), F32),
            jax.ShapeDtypeStruct((2, width), F32),
        ],
        compiler_params=pltpu.CompilerParams(vmem_limit_bytes=48 * 2**20),
        cost_estimate=pl.CostEstimate(
            flops=6 * count * width * width,
            bytes_accessed=16 * count * width + 6 * width * width,
            transcendentals=0,
        ),
        name="input_gradient",
    )(tokens, dr, dq, dk, dv, vecs, wq, wk, wv)


def body(
    tokens, norm_gain, norm_shift, query_weight, query_bias, key_weight, value_weight, value_bias,
    output_weight, output_bias, second_gain, second_shift, up_weight, up_bias, down_weight,
    down_bias, cotangent,
):
    width = tokens.shape[1]
    share = query_weight.shape[0]
    devices = width // share
    fan = up_weight.shape[1] // width

    small = jnp.concatenate(
        [norm_gain, norm_shift, query_bias, value_bias, output_bias, second_gain, second_shift, down_bias, up_bias]
    )
    small = jnp.pad(small, (0, width - small.shape[0]))[None]
    early = jnp.concatenate([query_weight, key_weight, value_weight, small])
    early = lax.all_gather(early, "dp", axis=0)
    up_tall = up_weight.reshape(share, fan, width).transpose(1, 0, 2).reshape(fan * share, width)
    late = jnp.concatenate([output_weight, down_weight, up_tall])
    late = lax.all_gather(late, "dp", axis=0)

    wq, wk, wv = (
        early[:, place * share : (place + 1) * share].reshape(width, width) for place in range(3)
    )
    small = early[:, 3 * share]
    vecs = (
        small[:, : 8 * share].reshape(devices, 8, share).transpose(1, 0, 2).reshape(8, width).astype(F32)
    )
    up_bias_all = small[:, 8 * share : (8 + fan) * share].reshape(1, fan * width).astype(F32)
    wo = late[:, :share].reshape(width, width)
    wd = late[:, share : (1 + fan) * share].reshape(fan * width, width)
    wu = (
        late[:, (1 + fan) * share :]
        .reshape(devices, fan, share, width)
        .transpose(1, 0, 2, 3)
        .reshape(fan * width, width)
    )

    h, q, k, v = project(tokens, vecs, wq, wk, wv)
    attn, lse = attend(q, k, v)
    mixed, dr, d_attn, vec_sums, up_bias_sum, g_wo, g_wu, g_wd = feed(
        tokens, attn, cotangent, vecs, up_bias_all, wo, wu, wd
    )
    late = jnp.concatenate(
        [
            g_wo.reshape(devices, share, width),
            g_wd.reshape(devices, fan * share, width),
            g_wu.reshape(fan, devices, share, width).transpose(1, 0, 2, 3).reshape(devices, fan * share, width),
        ],
        axis=1,
    )
    late = lax.psum_scatter(late, "dp", scatter_dimension=0)

    dq, dk, dv, bias_sums = attend_back(q, k, v, d_attn, lse)
    input_grad, norm_sums = input_gradient(tokens, dr, dq, dk, dv, vecs, wq, wk, wv)
    bias_sums = jnp.sum(bias_sums, axis=0)
    sums = jnp.concatenate([norm_sums, bias_sums, vec_sums])
    sums = sums.reshape(8, devices, share).transpose(1, 0, 2).reshape(devices, 8 * share)
    sums = jnp.concatenate([sums, up_bias_sum.reshape(devices, fan * share)], axis=1)
    sums = jnp.pad(sums, ((0, 0), (0, width - sums.shape[1])))
    early = jnp.concatenate(
        [dot_tn(h, part).astype(BF16).reshape(devices, share, width) for part in (dq, dk, dv)]
        + [sums.astype(BF16)[:, None]],
        axis=1,
    )
    early = lax.psum_scatter(early, "dp", scatter_dimension=0).astype(F32)
    late = late.astype(F32)
    g_wq, g_wk, g_wv = (early[place * share : (place + 1) * share] for place in range(3))
    sums = early[3 * share]
    vec_grads = [sums[place * share : (place + 1) * share] for place in range(8)]
    g_up_bias = sums[8 * share : (8 + fan) * share]
    g_wu = late[(1 + fan) * share :].reshape(fan, share, width).transpose(1, 0, 2).reshape(share, fan * width)
    return (
        mixed, input_grad,
        vec_grads[0], vec_grads[1], g_wq, vec_grads[2], g_wk, g_wv, vec_grads[3],
        late[:share], vec_grads[4], vec_grads[5], vec_grads[6],
        g_wu, g_up_bias, late[share : (1 + fan) * share], vec_grads[7],
    )


def solution(mesh):
    row, vec = P("dp", None), P("dp")
    params = (vec, vec, row, vec, row, row, vec, row, vec, vec, vec, row, vec, row, vec)
    return jax.shard_map(
        body,
        mesh=mesh,
        in_specs=(row, *params, row),
        out_specs=(row, row, *params),
        check_vma=False,
    )
```

```python
import functools

import jax
import jax.numpy as jnp
from jax import lax
from jax.experimental import pallas as pl
from jax.experimental.pallas import tpu as pltpu
from jax.sharding import PartitionSpec as P

HD = 64
SEQ = 1024
LANES = 128
QUERY_BLOCK = 256
F32 = jnp.float32
BF16 = jnp.bfloat16
EPSILON = 1e-05
GELU_SCALE = 0.7978845608028654
GELU_CUBIC = 0.044715


def dot_nn(left, right):
    return lax.dot_general(left, right, (((1,), (0,)), ((), ())), preferred_element_type=F32)


def dot_nt(left, right):
    return lax.dot_general(left, right, (((1,), (1,)), ((), ())), preferred_element_type=F32)


def dot_tn(left, right):
    return lax.dot_general(left, right, (((0,), (0,)), ((), ())), preferred_element_type=F32)


def normalise(values):
    center = values - jnp.mean(values, axis=-1, keepdims=True)
    rstd = lax.rsqrt(jnp.mean(center * center, axis=-1, keepdims=True) + EPSILON)
    return center * rstd, rstd


def whole(shape):
    return pl.BlockSpec(shape, lambda *_: (0,) * len(shape), pipeline_mode=pl.Buffered(1))


def rows(block, width):
    return pl.BlockSpec((block, width), lambda i: (i, 0))


GRID = (4, 2, 2)


def load_parts(spots, parts, held, sems, swap=None):
    half = held.shape[-1] // 2
    core = spots[2] if swap is None else 0
    copies = []
    for refs, axis, first, unit_rows in parts:
        place = spots[axis - 1]
        cols = refs[0].shape[-1]
        for order, ref in enumerate(refs):
            spot = place if order % 2 == 0 else 1 - place
            side = core if order < 2 else 1 - core
            start = side * half + first
            if not isinstance(start, int):
                start = pl.multiple_of(start, LANES)
            lanes = pl.ds(start, cols)
            source = ref.at[:, :, pl.ds(0, unit_rows), :]
            if axis == 1:
                target = held.at[:, spot, :, :, lanes]
            else:
                target = held.at[:, :, spot, :, lanes]
            copies.append(pltpu.make_async_copy(source, target, sems.at[len(copies)]))
    return copies


SMEM_SPEC = pl.BlockSpec(memory_space=pltpu.SMEM)
ANY_SPEC = pl.BlockSpec(memory_space=pl.ANY)


def early_parts(refs):
    return [(refs[0:4], 2, 0, 48), (refs[4:8], 1, 640, 48)]


def project_kernel(*args):
    spots, x_ref, vec_ref = args[:3]
    refs, (h_ref, q_ref, k_ref, v_ref, w, sem) = args[3:11], args[11:]

    @pl.when(pl.program_id(0) == 0)
    def _():
        copies = load_parts(spots, early_parts(refs), w, sem)
        for copy in copies:
            copy.start()
        for copy in copies:
            copy.wait()

    width = x_ref.shape[1]
    half = width // 2
    normed, _ = normalise(x_ref[...].astype(F32))
    h = (normed * vec_ref[0:1, :] + vec_ref[1:2, :]).astype(BF16)
    h_ref[...] = h
    for side in range(2):
        weight = w[:, :, :, :, side * 3 * half : (side + 1) * 3 * half].reshape(width, 3 * half)
        out = dot_nn(h, weight)
        cols = slice(side * half, (side + 1) * half)
        q = (out[:, :half] + vec_ref[2:3, cols]).astype(BF16)
        q_ref[:, cols] = (q.astype(F32) * HD**-0.5).astype(BF16)
        k_ref[:, cols] = out[:, half : 2 * half].astype(BF16)
        v_ref[:, cols] = (out[:, 2 * half :] + vec_ref[3:4, cols]).astype(BF16)


def project(spots, tokens, vecs, raw):
    count, width = tokens.shape
    block = 512
    out = jax.ShapeDtypeStruct((count, width), BF16)
    return pl.pallas_call(
        project_kernel,
        grid=(count // block,),
        in_specs=[SMEM_SPEC, rows(block, width), whole(vecs.shape)] + [ANY_SPEC] * 8,
        out_specs=[rows(block, width)] * 4,
        out_shape=[out] * 4,
        scratch_shapes=[pltpu.VMEM(GRID + (48, 3 * width), BF16), pltpu.SemaphoreType.DMA((8,))],
        compiler_params=pltpu.CompilerParams(vmem_limit_bytes=48 * 2**20),
        cost_estimate=pl.CostEstimate(
            flops=6 * count * width * width,
            bytes_accessed=10 * count * width + 6 * width * width,
            transcendentals=0,
        ),
        name="project",
    )(spots, tokens, vecs, *raw)


def head_only(values, head):
    lane = lax.broadcasted_iota(jnp.int32, values.shape, 1)
    keep = (lane < HD) if head == 0 else (lane >= HD)
    return jnp.where(keep, values, jnp.zeros_like(values))


def causal_t(scores_t):
    key = lax.broadcasted_iota(jnp.int32, scores_t.shape, 0)
    query = lax.broadcasted_iota(jnp.int32, scores_t.shape, 1)
    return key <= query


def attend_kernel(q_ref, k_ref, v_ref, o_ref, lse_ref, out_t):
    seq_len = q_ref.shape[0]
    k = k_ref[...]
    v_t = v_ref[...].astype(F32).T.astype(BF16)
    for head in range(2):
        q = head_only(q_ref[...], head)
        v_head = v_t[head * HD : (head + 1) * HD, :]
        for start in range(0, seq_len, QUERY_BLOCK):
            end = start + QUERY_BLOCK
            q_part = q[start:end]
            diag = dot_nt(k[start:end], q_part)
            diag = jnp.where(causal_t(diag), diag, -jnp.inf)
            peak = jnp.max(diag, axis=0, keepdims=True)
            if start:
                full = dot_nt(k[:start], q_part)
                peak = jnp.maximum(peak, jnp.max(full, axis=0, keepdims=True))
            p_diag = jnp.exp(diag - peak)
            total = jnp.sum(p_diag, axis=0, keepdims=True)
            mixed = dot_nn(v_head[:, start:end], p_diag.astype(BF16))
            if start:
                p_full = jnp.exp(full - peak)
                total = total + jnp.sum(p_full, axis=0, keepdims=True)
                mixed = mixed + dot_nn(v_head[:, :start], p_full.astype(BF16))
            out_t[head * HD : (head + 1) * HD, start:end] = mixed * (1.0 / total)
            lse_ref[0, 0, head : head + 1, start:end] = peak + jnp.log(total)
    o_ref[...] = out_t[...].T.astype(BF16)


def attend(q, k, v):
    count, width = q.shape
    seqs, pairs = count // SEQ, width // LANES
    block = pl.BlockSpec((SEQ, LANES), lambda s, p: (s, p))
    return pl.pallas_call(
        attend_kernel,
        grid=(seqs, pairs),
        in_specs=[block] * 3,
        out_specs=[block, pl.BlockSpec((1, 1, 2, SEQ), lambda s, p: (s, p, 0, 0))],
        out_shape=[
            jax.ShapeDtypeStruct((count, width), BF16),
            jax.ShapeDtypeStruct((seqs, pairs, 2, SEQ), F32),
        ],
        scratch_shapes=[pltpu.VMEM((LANES, SEQ), F32)],
        compiler_params=pltpu.CompilerParams(vmem_limit_bytes=48 * 2**20),
        cost_estimate=pl.CostEstimate(
            flops=4 * count * SEQ * width,
            bytes_accessed=8 * count * width,
            transcendentals=count * SEQ * width // HD,
        ),
        name="attend",
    )(q, k, v)


def attend_back_kernel(
    side_ref, q_ref, k_ref, v_ref, do_ref, lse_ref, out_ref, sums_ref, dq_t, dk_acc, dv_acc
):
    seq_len = q_ref.shape[0]
    k = k_ref[...]
    v = v_ref[...]
    k_t = k.astype(F32).T.astype(BF16)
    dk_acc[...] = jnp.zeros_like(dk_acc)
    dv_acc[...] = jnp.zeros_like(dv_acc)
    for head in range(2):
        q = head_only(q_ref[...], head)
        do = head_only(do_ref[...], head)
        k_head = k_t[head * HD : (head + 1) * HD, :]
        for start in range(0, seq_len, QUERY_BLOCK):
            end = start + QUERY_BLOCK
            q_part = q[start:end]
            do_part = do[start:end]
            lse = lse_ref[0, 0, head : head + 1, start:end]
            scores = dot_nt(k[start:end], q_part)
            p_diag = jnp.exp(jnp.where(causal_t(scores), scores, -jnp.inf) - lse)
            dp_diag = dot_nt(v[start:end], do_part)
            inner = jnp.sum(p_diag * dp_diag, axis=0, keepdims=True)
            if start:
                p_full = jnp.exp(dot_nt(k[:start], q_part) - lse)
                dp_full = dot_nt(v[:start], do_part)
                inner = inner + jnp.sum(p_full * dp_full, axis=0, keepdims=True)
                ds_full = (p_full * (dp_full - inner)).astype(BF16)
                dv_acc[:start, :] += dot_nn(p_full.astype(BF16), do_part)
                dk_acc[:start, :] += dot_nn(ds_full, q_part)
            ds_diag = (p_diag * (dp_diag - inner)).astype(BF16)
            dv_acc[start:end, :] += dot_nn(p_diag.astype(BF16), do_part)
            dk_acc[start:end, :] += dot_nn(ds_diag, q_part)
            dq = dot_nn(k_head[:, start:end], ds_diag)
            if start:
                dq = dq + dot_nn(k_head[:, :start], ds_full)
            dq_t[head * HD : (head + 1) * HD, start:end] = dq
    dq = (dq_t[...].T * HD**-0.5).astype(BF16)
    dv = dv_acc[...].astype(BF16)
    out_ref[0] = dq
    out_ref[1] = dk_acc[...].astype(BF16)
    out_ref[2] = dv
    sums_ref[0, 0:1, :] = jnp.sum(dq.astype(F32), axis=0, keepdims=True)
    sums_ref[0, 1:2, :] = jnp.sum(dv.astype(F32), axis=0, keepdims=True)


def attend_back(where, q, k, v, d_attn, lse):
    width = q.shape[1]
    pairs = width // LANES // 2
    block = pl.BlockSpec((SEQ, LANES), lambda p, at: (at[0], at[1] * pairs + p))
    return pl.pallas_call(
        attend_back_kernel,
        grid_spec=pltpu.PrefetchScalarGridSpec(
            num_scalar_prefetch=1,
            grid=(pairs,),
            in_specs=[block] * 4
            + [pl.BlockSpec((1, 1, 2, SEQ), lambda p, at: (at[0], at[1] * pairs + p, 0, 0))],
            out_specs=[
                pl.BlockSpec((3, SEQ, LANES), lambda p, at: (0, 0, p)),
                pl.BlockSpec((1, 2, LANES), lambda p, at: (0, 0, p)),
            ],
            scratch_shapes=[
                pltpu.VMEM((LANES, SEQ), F32),
                pltpu.VMEM((SEQ, LANES), F32),
                pltpu.VMEM((SEQ, LANES), F32),
            ],
        ),
        out_shape=[
            jax.ShapeDtypeStruct((3, SEQ, width // 2), BF16),
            jax.ShapeDtypeStruct((1, 2, width // 2), F32),
        ],
        compiler_params=pltpu.CompilerParams(vmem_limit_bytes=48 * 2**20),
        cost_estimate=pl.CostEstimate(
            flops=5 * SEQ * SEQ * width,
            bytes_accessed=7 * SEQ * width,
            transcendentals=SEQ * SEQ * width // HD // 2,
        ),
        name="attend_back",
    )(where, q, k, v, d_attn, lse)


def weight_grad_kernel(h_ref, *refs):
    grads, (first_ref, second_ref, total) = refs[:-3], refs[-3:]
    step = pl.program_id(0)
    per = pl.num_programs(0) // len(grads)

    @pl.when(step == 0)
    def _():
        total[...] = jnp.zeros_like(total)

    for place, ref in enumerate(grads):
        @pl.when(step // per == place)
        def _():
            total[...] += dot_tn(h_ref[...], jnp.concatenate([ref[0], ref[1], ref[2]], axis=1))

    @pl.when(step == pl.num_programs(0) - 1)
    def _():
        cut = first_ref.shape[1]
        first_ref[...] = total[:, :cut].astype(BF16)
        second_ref[...] = total[:, cut:].astype(BF16)


def weight_grad(h, grads):
    count, width = h.shape
    block = 512
    per = SEQ // block
    cut = 640
    cols = 3 * width // 2

    def spec(place):
        return pl.BlockSpec(
            (3, block, width // 2), lambda i: (0, jnp.clip(i - place * per, 0, per - 1), 0)
        )

    return pl.pallas_call(
        weight_grad_kernel,
        grid=(count // block,),
        in_specs=[rows(block, width)] + [spec(place) for place in range(len(grads))],
        out_specs=[whole((width, cut)), whole((width, cols - cut))],
        out_shape=[
            jax.ShapeDtypeStruct((width, cut), BF16),
            jax.ShapeDtypeStruct((width, cols - cut), BF16),
        ],
        scratch_shapes=[pltpu.VMEM((width, cols), F32)],
        compiler_params=pltpu.CompilerParams(vmem_limit_bytes=48 * 2**20),
        cost_estimate=pl.CostEstimate(
            flops=2 * count * width * cols,
            bytes_accessed=2 * count * (width + cols) + 2 * width * cols,
            transcendentals=0,
        ),
        name="weight_grad",
    )(h, *grads)


LATE_ROWS = 432


def late_parts(packed, wd, wuo, side):
    half = packed.shape[-1]

    def lanes(start):
        return pl.ds(start if isinstance(start, int) else pl.multiple_of(start, LANES), half)

    yield packed.at[:, pl.ds(0, 192), :], wd.at[:, :, lanes(side * half)]
    for block in range(5):
        yield packed.at[:, pl.ds(192 + 48 * block, 48), :], wuo.at[:, :, lanes((side * 5 + block) * half)]


def feed_kernel(*args):
    spots, x_ref, a_ref, dy_ref, vec_ref, ub_ref, late_ref = args[:7]
    mixed_ref, dr_ref, da_ref, gvec_ref, gub_ref, keep_ref, send_ref = args[7:14]
    wd, wuo, acc_d, acc_uo, sem = args[14:]
    step = pl.program_id(0)
    width = x_ref.shape[1]
    up_half = wuo.shape[-1] // 2
    out_first = up_half - width // 2

    def flat(values):
        return values.reshape(width, values.shape[-1])

    def out_weight():
        return jnp.concatenate(
            [flat(wuo[:, :, end - width // 2 : end]) for end in (up_half, 2 * up_half)], axis=1
        )

    @pl.when(step == 0)
    def _():
        copies = []
        for side in range(2):
            for part in late_parts(late_ref.at[:, side], wd, wuo, side):
                copies.append(pltpu.make_async_copy(*part, sem.at[len(copies)]))
                copies[-1].start()
        acc_d[...] = jnp.zeros_like(acc_d)
        acc_uo[...] = jnp.zeros_like(acc_uo)
        gvec_ref[...] = jnp.zeros_like(gvec_ref)
        gub_ref[...] = jnp.zeros_like(gub_ref)
        for copy in copies:
            copy.wait()

    attn = a_ref[...]
    dy = dy_ref[...]
    dy_wide = dy.astype(F32)
    resid = x_ref[...].astype(F32) + dot_nn(attn, out_weight()) + vec_ref[4:5, :]
    normed, rstd = normalise(resid)
    gain = vec_ref[5:6, :]
    h2 = (normed * gain + vec_ref[6:7, :]).astype(BF16)

    def chunk(index, carry):
        mixed, dh2 = carry
        cols = pl.ds(pl.multiple_of(index * width, width), width)
        up_cols = pl.ds(pl.multiple_of(index * width + index // 2 * (width // 2), LANES), width)
        up = flat(wuo[:, :, up_cols])
        down = wd[pl.ds(index * 4, 4)].reshape(width, width)
        u = dot_nn(h2, up) + ub_ref[:, cols]
        d_act = dot_nt(dy, down)
        square = u * u
        tanh = jnp.tanh(GELU_SCALE * u * (1.0 + GELU_CUBIC * square))
        half = 0.5 + 0.5 * tanh
        act = (u * half).astype(BF16)
        slope = half + u * (0.5 - 0.5 * tanh * tanh) * (
            GELU_SCALE * (1.0 + 3.0 * GELU_CUBIC * square)
        )
        du = (d_act * slope).astype(BF16)
        gub_ref[:, cols] += jnp.sum(du.astype(F32), axis=0, keepdims=True)
        acc_d[cols, :] += dot_tn(act, dy)
        acc_uo[:, up_cols] += dot_tn(h2, du)
        return (mixed + dot_nn(act, down), dh2 + dot_nt(du, up))

    mixed, dh2 = lax.fori_loop(
        0, wd.shape[0] // 4, chunk, (resid + vec_ref[7:8, :], jnp.zeros_like(resid))
    )
    mixed_ref[...] = mixed.astype(BF16)
    g = dh2 * gain
    dr = dy_wide + rstd * (
        g
        - jnp.mean(g, axis=-1, keepdims=True)
        - normed * jnp.mean(g * normed, axis=-1, keepdims=True)
    )
    dr_ref[...] = dr
    da = dr.astype(BF16)
    da_ref[...] = dot_nt(da, out_weight()).astype(BF16)
    g_out = dot_tn(attn, da)
    acc_uo[:, out_first:up_half] += g_out[:, : width // 2]
    acc_uo[:, up_half + out_first :] += g_out[:, width // 2 :]
    gvec_ref[0:1, :] += jnp.sum(da.astype(F32), axis=0, keepdims=True)
    gvec_ref[1:2, :] += jnp.sum(dh2 * normed, axis=0, keepdims=True)
    gvec_ref[2:3, :] += jnp.sum(dh2, axis=0, keepdims=True)
    gvec_ref[3:4, :] += jnp.sum(dy_wide, axis=0, keepdims=True)

    @pl.when(step == pl.num_programs(0) - 1)
    def _():
        core = spots[2]
        copies = []
        wd[...] = acc_d[...].astype(BF16).reshape(wd.shape)
        wuo[...] = acc_uo[...].astype(BF16).reshape(wuo.shape)
        for side, out in ((1 - core, send_ref), (core, keep_ref)):
            for there, here in late_parts(out, wd, wuo, side):
                copies.append(pltpu.make_async_copy(here, there, sem.at[len(copies)]))
                copies[-1].start()
        for copy in copies:
            copy.wait()


def feed(spots, tokens, attn, cotangent, vecs, up_bias, late):
    count, width = tokens.shape
    fan = up_bias.shape[1]
    block = 512
    down, up = (16, 192, width), (16, 48, width + fan)
    half = (16, LATE_ROWS, width // 2)
    size = 2 * width * fan + width * width
    return pl.pallas_call(
        feed_kernel,
        grid=(count // block,),
        in_specs=[SMEM_SPEC] + [rows(block, width)] * 3 + [whole(vecs.shape), whole(up_bias.shape), ANY_SPEC],
        out_specs=[rows(block, width)] * 3 + [whole((4, width)), whole(up_bias.shape)] + [ANY_SPEC] * 2,
        out_shape=[
            jax.ShapeDtypeStruct((count, width), BF16),
            jax.ShapeDtypeStruct((count, width), F32),
            jax.ShapeDtypeStruct((count, width), BF16),
            jax.ShapeDtypeStruct((4, width), F32),
            jax.ShapeDtypeStruct(up_bias.shape, F32),
        ] + [jax.ShapeDtypeStruct(half, BF16)] * 2,
        scratch_shapes=[
            pltpu.VMEM(down, BF16),
            pltpu.VMEM(up, BF16),
            pltpu.VMEM((fan, width), F32),
            pltpu.VMEM((width, width + fan), F32),
            pltpu.SemaphoreType.DMA((12,)),
        ],
        compiler_params=pltpu.CompilerParams(vmem_limit_bytes=60 * 2**20),
        cost_estimate=pl.CostEstimate(
            flops=6 * count * size,
            bytes_accessed=14 * count * width + 4 * size,
            transcendentals=count * fan,
        ),
        name="feed",
    )(spots, tokens, attn, cotangent, vecs, up_bias, late)


def input_grad_kernel(*args):
    spots, x_ref, dr_ref, keep_ref, send_ref, vec_ref = args[:6]
    refs, (ig_ref, sums_ref, w, sem) = args[6:14], args[-4:]

    @pl.when(pl.program_id(0) == 0)
    def _():
        copies = load_parts(spots, early_parts(refs), w, sem, swap=True)
        for copy in copies:
            copy.start()
        sums_ref[...] = jnp.zeros_like(sums_ref)
        for copy in copies:
            copy.wait()

    width = x_ref.shape[1]
    half = width // 2
    normed, rstd = normalise(x_ref[...].astype(F32))
    dh = jnp.zeros(x_ref.shape, F32)
    for side, ref in enumerate((keep_ref, send_ref)):
        grads = jnp.concatenate([ref[0], ref[1], ref[2]], axis=1)
        dh = dh + dot_nt(
            grads, w[:, :, :, :, side * 3 * half : (side + 1) * 3 * half].reshape(width, 3 * half)
        )
    g = dh * vec_ref[0:1, :]
    ig_ref[...] = dr_ref[...] + rstd * (
        g
        - jnp.mean(g, axis=-1, keepdims=True)
        - normed * jnp.mean(g * normed, axis=-1, keepdims=True)
    )
    sums_ref[0:1, :] += jnp.sum(dh * normed, axis=0, keepdims=True)
    sums_ref[1:2, :] += jnp.sum(dh, axis=0, keepdims=True)


def input_gradient(spots, tokens, dr, keep, send, vecs, raw, seq, filled=None):
    count, width = tokens.shape
    block = 512
    steps = SEQ // block
    part = pl.BlockSpec((block, width), lambda i: (seq * steps + i, 0))
    third = pl.BlockSpec((3, block, width // 2), lambda i: (0, i, 0))
    extra = [] if filled is None else [filled]
    return pl.pallas_call(
        input_grad_kernel,
        grid=(steps,),
        in_specs=[SMEM_SPEC, part, part, third, third, whole(vecs.shape)] + [ANY_SPEC] * (8 + len(extra)),
        out_specs=[part, whole((2, width))],
        out_shape=[
            jax.ShapeDtypeStruct((count, width), F32),
            jax.ShapeDtypeStruct((2, width), F32),
        ],
        input_output_aliases={14: 0} if extra else {},
        scratch_shapes=[pltpu.VMEM(GRID + (48, 3 * width), BF16), pltpu.SemaphoreType.DMA((8,))],
        compiler_params=pltpu.CompilerParams(vmem_limit_bytes=48 * 2**20),
        cost_estimate=pl.CostEstimate(
            flops=6 * SEQ * width * width,
            bytes_accessed=16 * SEQ * width + 6 * width * width,
            transcendentals=0,
        ),
        name="input_gradient",
    )(spots, tokens, dr, keep, send, vecs, *raw, *extra)


def take(values, index, axis):
    return lax.dynamic_index_in_dim(values, index, axis, keepdims=False)


def wide(values):
    return values.astype(F32)


class Chips:
    def __init__(self):
        me = lax.axis_index("dp")
        self.core = me % 2
        self.strides = (8, 4, 2)
        self.spots = tuple((me // stride) % size for stride, size in zip(self.strides, GRID))

    def pair(self, values):
        return lax.ppermute(values, "dp", [(i, i ^ 1) for i in range(32)])

    def swap(self, values, axis):
        stride = self.strides[axis]
        return lax.ppermute(values, "dp", [(i, i ^ stride) for i in range(32)])

    def turn(self, values, step):
        size, stride = GRID[0], self.strides[0]
        return lax.ppermute(values, "dp", [(i, (i + step * stride) % (size * stride)) for i in range(32)])

    def both(self, spot, own, other, axis):
        return jnp.where(spot == 0, jnp.stack([own, other], axis), jnp.stack([other, own], axis))

    def gather_z(self, own):
        size, spot = GRID[0], self.spots[0]
        seen = [own] + [self.turn(own, step) for step in range(1, size)]
        slots = [lax.select_n(spot, *[seen[(q - p) % size] for q in range(size)]) for p in range(size)]
        return jnp.stack(slots)

    def gather(self, unit, last):
        if last == 2:
            units = self.both(self.spots[1], unit, self.swap(unit, 1), 0)
            units = self.gather_z(units)
        else:
            units = self.gather_z(unit)
            units = self.both(self.spots[2], units, self.swap(units, 2), 1)
        other = self.swap(units, last)
        return [units, other, self.pair(units), self.pair(other)]

    def away(self, terms, axis, at, wire):
        return sum(wide(take(term, 1 - self.spots[axis], at)) for term in terms).astype(wire)

    def fold(self, terms, axis, at, wire, away=None):
        away = self.away(terms, axis, at, wire) if away is None else away
        return sum(wide(take(term, self.spots[axis], at)) for term in terms) + wide(self.swap(away, axis))

    def fold_z(self, values, wire):
        size, spot = GRID[0], self.spots[0]
        total = wide(take(values, spot, 0))
        for step in range(1, size):
            away = take(values, (spot + step) % size, 0).astype(wire)
            total = total + wide(self.turn(away, step))
        return total

    def reduce(self, terms, first, wire, away=None):
        if first == 2:
            total = self.fold_z(self.fold(terms, 2, 2, wire, away), wire)
            return self.fold([total], 1, 0, wire)
        total = self.fold(terms, 1, 1, wire, away)
        total = self.fold([total], 2, 1, wire)
        return self.fold_z(total, wire)

    def finish(self, unit):
        share = unit.shape[0] // 2
        mine = lax.dynamic_slice_in_dim(unit, self.core * share, share, 0)
        other = self.pair(lax.dynamic_slice_in_dim(unit, (1 - self.core) * share, share, 0))
        return [jnp.where(self.core == 0, mine, other), jnp.where(self.core == 0, other, mine)]


def halves(parts):
    return [
        jnp.concatenate([part[:, side * part.shape[1] // 2 : (side + 1) * part.shape[1] // 2] for part in parts], axis=1)
        for side in range(2)
    ]


def join(sides, first, last):
    return jnp.concatenate([side[:, first:last] for side in sides], axis=1)


def pack_late(down, up):
    return jnp.concatenate([down] + jnp.split(up, 5, axis=-1), axis=-2)


def unpack_late(packed):
    down, *up = jnp.split(packed, [192, 240, 288, 336, 384], axis=-2)
    return down, jnp.concatenate(up, axis=-1)


def gather_all(chips, shards, small):
    if chips is None:
        early, up, down = (
            jnp.concatenate(halves([lax.all_gather(s, "dp", axis=0, tiled=True) for s in part]), axis=1)
            for part in shards
        )
        small = lax.all_gather(small, "dp", axis=0)

        def parts(axis, first, last):
            unit = early.reshape(GRID + (48, -1))
            cols = unit.shape[-1] // 2
            return [
                take(unit, place, axis)[..., side * cols + first : side * cols + last]
                for side in range(2) for place in range(2)
            ]

        late = jnp.stack(
            [
                pack_late(*(w.reshape(16, -1, 2, w.shape[1] // 2)[:, :, side] for w in (down, up)))
                for side in range(2)
            ],
            axis=1,
        )
        return parts(2, 0, 640) + parts(1, 640, 1152), late, small
    units = []
    for part in shards:
        sides = halves(part)
        mine = jnp.where(chips.core == 0, sides[0], sides[1])
        other = chips.pair(jnp.where(chips.core == 0, sides[1], sides[0]))
        units.append(
            jnp.where(chips.core == 0, jnp.concatenate([mine, other]), jnp.concatenate([other, mine]))
        )
    early_unit, up_unit, down_unit = units
    late = lax.all_gather(pack_late(down_unit, up_unit), "dp", axis=0)
    late = late.reshape(16, 2, LATE_ROWS, -1)
    early = chips.gather(early_unit[:, :640], 2) + chips.gather(
        jnp.concatenate([early_unit[:, 640:], small]), 1
    )
    seen = [part[:, :, 48:] for part in early[4:]]
    small = chips.both(
        chips.core,
        chips.both(chips.spots[1], seen[0], seen[1], 1),
        chips.both(chips.spots[1], seen[2], seen[3], 1),
        3,
    )
    return early, late, small.reshape((32,) + small.shape[4:])


def tie(*values):
    return lax.optimization_barrier(values)


def reduce_small(chips, sums):
    if chips is None:
        return lax.psum_scatter(sums, "dp", scatter_dimension=0)
    sums = sums.reshape(GRID + (2, -1))
    other = chips.pair(take(sums, 1 - chips.core, 3))
    return chips.reduce([take(sums, chips.core, 3) + other], 2, F32)


def body(
    tokens, norm_gain, norm_shift, query_weight, query_bias, key_weight, value_weight, value_bias,
    output_weight, output_bias, second_gain, second_shift, up_weight, up_bias, down_weight,
    down_bias, cotangent,
):
    width = tokens.shape[1]
    share = query_weight.shape[0]
    devices = width // share
    fan = up_weight.shape[1]
    half = width // 2
    chips = Chips() if devices == 32 else None
    core = jnp.int32(0) if chips is None else chips.core
    spots = jnp.stack([core, core, core] if chips is None else [chips.spots[1], chips.spots[2], core])

    small = (
        norm_gain, norm_shift, query_bias, value_bias, output_bias, second_gain, second_shift, down_bias, up_bias
    )
    small = sum(
        jnp.pad(values[None], ((row, 15 - row), (0, 512 - values.shape[0]))) for row, values in enumerate(small)
    )
    shards = ([query_weight, key_weight, value_weight], [up_weight, output_weight], [down_weight])
    early, late, small = gather_all(chips, shards, small)
    vecs = wide(
        small[:, :8, :share].transpose(1, 0, 2).reshape(8, width)
    )
    up_bias_all = wide(small[:, 8, : fan // devices].reshape(1, fan))

    h, q, k, v = project(spots, tokens, vecs, early)
    attn, lse = attend(q, k, v)
    mixed, dr, d_attn, vec_sums, up_bias_sum, late_keep, late_send = feed(
        spots, tokens, attn, cotangent, vecs, up_bias_all, late
    )

    seqs = tokens.shape[0] // SEQ

    def back(side, seq, operand):
        where = jnp.stack([jnp.int32(seq), side])
        return attend_back(where, operand, k, v, d_attn, lse)

    def grid(values):
        return values.reshape(GRID + (48, values.shape[-1]))

    if chips is None:
        sends = [back(1 - core, seq, q) for seq in range(seqs)]
        keeps = [back(core, seq, q) for seq in range(seqs)]
        early_send, early_keep = (
            jnp.concatenate(weight_grad(h, [part[0] for part in parts]), axis=1) for parts in (sends, keeps)
        )
        late = [unpack_late(side) for side in (late_keep, late_send)]
        g_down, g_up, g_early = (
            jnp.split(
                wide(
                    lax.psum_scatter(
                        jnp.concatenate([side.reshape(-1, side.shape[-1]) for side in sides], axis=1),
                        "dp", scatter_dimension=0, tiled=True,
                    )
                ),
                2, axis=1,
            )
            for sides in (
                [side[0] for side in late], [side[1] for side in late], [early_keep, early_send]
            )
        )
        input_grad, norm_sums = None, 0.0
        for seq in range(seqs):
            input_grad, more = input_gradient(
                spots, tokens, dr, keeps[seq][0], sends[seq][0], vecs, early, seq, input_grad
            )
            norm_sums = norm_sums + more
    else:
        sends = [back(1 - core, 0, q)]
        late_total = (wide(late_keep) + wide(chips.pair(late_send))).astype(BF16)
        late_total, q = tie(late_total, q)
        late_total = lax.psum_scatter(
            late_total, "dp", scatter_dimension=0, axis_index_groups=[list(range(c, 32, 2)) for c in range(2)]
        )
        sends += [back(1 - core, seq, q) for seq in range(1, seqs)]
        early_send = weight_grad(h, [part[0] for part in sends])
        *early_send, q = tie(*early_send, q)
        early_other = [chips.pair(part) for part in early_send]
        keeps = [back(core, seq, q) for seq in range(seqs)]
        early_keep = weight_grad(h, [part[0] for part in keeps])
        terms = [[grid(own), grid(other)] for own, other in zip(early_keep, early_other)]
        away = [chips.away(terms[0], 2, 2, BF16), chips.away(terms[1], 1, 1, BF16)]
        *away, first = tie(*away, keeps[0][0])
        input_grad, norm_sums = input_gradient(spots, tokens, dr, first, sends[0][0], vecs, early, 0)
        totals = [chips.fold(terms[0], 2, 2, BF16, away[0]), chips.fold(terms[1], 1, 1, BF16, away[1])]
        *totals, last = tie(*totals, keeps[-1][0])
        for seq in range(1, seqs):
            input_grad, more = input_gradient(
                spots, tokens, dr, last if seq == seqs - 1 else keeps[seq][0], sends[seq][0], vecs, early, seq, input_grad
            )
            norm_sums = norm_sums + more
        first = chips.fold([chips.fold_z(totals[0], BF16)], 1, 0, BF16)
        second = chips.fold_z(chips.fold([totals[1]], 2, 1, BF16), BF16)
        g_early = chips.finish(jnp.concatenate([first, second], axis=1))
        down, up = unpack_late(wide(late_total))
        g_down, g_up = chips.finish(down), chips.finish(up)
    sums_keep, sums_send = (sum(part[1][0] for part in parts) for parts in (keeps, sends))
    bias_sums = jnp.where(
        core == 0,
        jnp.concatenate([sums_keep, sums_send], axis=1),
        jnp.concatenate([sums_send, sums_keep], axis=1),
    )
    sums = jnp.concatenate([norm_sums, bias_sums, vec_sums])
    sums = sums.reshape(8, devices, share).transpose(1, 0, 2).reshape(devices, 8 * share)
    sums = jnp.concatenate([sums, up_bias_sum.reshape(devices, fan * share // width)], axis=1)
    sums = reduce_small(chips, sums)
    vec_grads = [sums[place * share : (place + 1) * share] for place in range(8)]
    g_wq, g_wk, g_wv = (join(g_early, place * half, (place + 1) * half) for place in range(3))
    return (
        mixed, input_grad,
        vec_grads[0], vec_grads[1], g_wq, vec_grads[2], g_wk, g_wv, vec_grads[3],
        join(g_up, fan // 2, (fan + width) // 2), vec_grads[4], vec_grads[5], vec_grads[6],
        join(g_up, 0, fan // 2), sums[8 * share :], join(g_down, 0, half), vec_grads[7],
    )


def solution(mesh):
    row, vec = P("dp", None), P("dp")
    params = (vec, vec, row, vec, row, row, vec, row, vec, vec, vec, row, vec, row, vec)
    return jax.shard_map(
        body,
        mesh=mesh,
        in_specs=(row, *params, row),
        out_specs=(row, row, *params),
        check_vma=False,
    )
```

```python
import functools

import jax
import jax.numpy as jnp
from jax import lax
from jax.experimental import pallas as pl
from jax.experimental.pallas import tpu as pltpu
from jax.sharding import PartitionSpec as P

HD = 64
SEQ = 1024
LANES = 128
FORWARD_BLOCK = 512
BACKWARD_BLOCK = 256
F32 = jnp.float32
BF16 = jnp.bfloat16
EPSILON = 1e-05
GELU_SCALE = 0.7978845608028654
GELU_CUBIC = 0.044715


def dot_nn(left, right):
    return lax.dot_general(left, right, (((1,), (0,)), ((), ())), preferred_element_type=F32)


def dot_nt(left, right):
    return lax.dot_general(left, right, (((1,), (1,)), ((), ())), preferred_element_type=F32)


def dot_tn(left, right):
    return lax.dot_general(left, right, (((0,), (0,)), ((), ())), preferred_element_type=F32)


def normalise(values):
    center = values - jnp.mean(values, axis=-1, keepdims=True)
    rstd = lax.rsqrt(jnp.mean(center * center, axis=-1, keepdims=True) + EPSILON)
    return center * rstd, rstd


def whole(shape):
    return pl.BlockSpec(shape, lambda *_: (0,) * len(shape), pipeline_mode=pl.Buffered(1))


def rows(block, width):
    return pl.BlockSpec((block, width), lambda i: (i, 0))


GRID = (4, 2, 2)


def load_parts(spots, parts, held, sems, swap=None):
    half = held.shape[-1] // 2
    core = spots[2] if swap is None else 0
    copies = []
    for refs, axis, first, unit_rows in parts:
        place = spots[axis - 1]
        cols = refs[0].shape[-1]
        for order, ref in enumerate(refs):
            spot = place if order % 2 == 0 else 1 - place
            side = core if order < 2 else 1 - core
            start = side * half + first
            if not isinstance(start, int):
                start = pl.multiple_of(start, LANES)
            lanes = pl.ds(start, cols)
            source = ref.at[:, :, pl.ds(0, unit_rows), :]
            if axis == 1:
                target = held.at[:, spot, :, :, lanes]
            else:
                target = held.at[:, :, spot, :, lanes]
            copies.append(pltpu.make_async_copy(source, target, sems.at[len(copies)]))
    return copies


SMEM_SPEC = pl.BlockSpec(memory_space=pltpu.SMEM)
ANY_SPEC = pl.BlockSpec(memory_space=pl.ANY)


def early_parts(refs):
    return [(refs[0:4], 2, 0, 48), (refs[4:8], 1, 640, 48)]


def project_kernel(*args):
    spots, x_ref, vec_ref = args[:3]
    refs, (h_ref, q_ref, k_ref, v_ref, w, sem) = args[3:11], args[11:]

    @pl.when(pl.program_id(0) == 0)
    def _():
        copies = load_parts(spots, early_parts(refs), w, sem)
        for copy in copies:
            copy.start()
        for copy in copies:
            copy.wait()

    width = x_ref.shape[1]
    half = width // 2
    normed, _ = normalise(x_ref[...].astype(F32))
    h = (normed * vec_ref[0:1, :] + vec_ref[1:2, :]).astype(BF16)
    h_ref[...] = h
    for side in range(2):
        weight = w[:, :, :, :, side * 3 * half : (side + 1) * 3 * half].reshape(width, 3 * half)
        out = dot_nn(h, weight)
        cols = slice(side * half, (side + 1) * half)
        q = (out[:, :half] + vec_ref[2:3, cols]).astype(BF16)
        q_ref[:, cols] = (q.astype(F32) * HD**-0.5).astype(BF16)
        k_ref[:, cols] = out[:, half : 2 * half].astype(BF16)
        v_ref[:, cols] = (out[:, 2 * half :] + vec_ref[3:4, cols]).astype(BF16)


def project(spots, tokens, vecs, raw):
    count, width = tokens.shape
    block = 512
    out = jax.ShapeDtypeStruct((count, width), BF16)
    return pl.pallas_call(
        project_kernel,
        grid=(count // block,),
        in_specs=[SMEM_SPEC, rows(block, width), whole(vecs.shape)] + [ANY_SPEC] * 8,
        out_specs=[rows(block, width)] * 4,
        out_shape=[out] * 4,
        scratch_shapes=[pltpu.VMEM(GRID + (48, 3 * width), BF16), pltpu.SemaphoreType.DMA((8,))],
        compiler_params=pltpu.CompilerParams(vmem_limit_bytes=48 * 2**20),
        cost_estimate=pl.CostEstimate(
            flops=6 * count * width * width,
            bytes_accessed=10 * count * width + 6 * width * width,
            transcendentals=0,
        ),
        name="project",
    )(spots, tokens, vecs, *raw)


def head_only(values, head):
    lane = lax.broadcasted_iota(jnp.int32, values.shape, 1)
    keep = (lane < HD) if head == 0 else (lane >= HD)
    return jnp.where(keep, values, jnp.zeros_like(values))


def causal_t(scores_t):
    key = lax.broadcasted_iota(jnp.int32, scores_t.shape, 0)
    query = lax.broadcasted_iota(jnp.int32, scores_t.shape, 1)
    return key <= query


def attend_kernel(q_ref, k_ref, v_ref, o_ref, lse_ref, out_t):
    seq_len = q_ref.shape[0]
    k = k_ref[...]
    v_t = v_ref[...].astype(F32).T.astype(BF16)
    for head in range(2):
        q = head_only(q_ref[...], head)
        v_head = v_t[head * HD : (head + 1) * HD, :]
        for start in range(0, seq_len, FORWARD_BLOCK):
            end = start + FORWARD_BLOCK
            q_part = q[start:end]
            diag = dot_nt(k[start:end], q_part)
            diag = jnp.where(causal_t(diag), diag, -jnp.inf)
            peak = jnp.max(diag, axis=0, keepdims=True)
            if start:
                full = dot_nt(k[:start], q_part)
                peak = jnp.maximum(peak, jnp.max(full, axis=0, keepdims=True))
            p_diag = jnp.exp(diag - peak)
            total = jnp.sum(p_diag, axis=0, keepdims=True)
            mixed = dot_nn(v_head[:, start:end], p_diag.astype(BF16))
            if start:
                p_full = jnp.exp(full - peak)
                total = total + jnp.sum(p_full, axis=0, keepdims=True)
                mixed = mixed + dot_nn(v_head[:, :start], p_full.astype(BF16))
            out_t[head * HD : (head + 1) * HD, start:end] = mixed * (1.0 / total)
            lse_ref[0, 0, head : head + 1, start:end] = peak + jnp.log(total)
    o_ref[...] = out_t[...].T.astype(BF16)


def attend(q, k, v):
    count, width = q.shape
    seqs, pairs = count // SEQ, width // LANES
    block = pl.BlockSpec((SEQ, LANES), lambda s, p: (s, p))
    return pl.pallas_call(
        attend_kernel,
        grid=(seqs, pairs),
        in_specs=[block] * 3,
        out_specs=[block, pl.BlockSpec((1, 1, 2, SEQ), lambda s, p: (s, p, 0, 0))],
        out_shape=[
            jax.ShapeDtypeStruct((count, width), BF16),
            jax.ShapeDtypeStruct((seqs, pairs, 2, SEQ), F32),
        ],
        scratch_shapes=[pltpu.VMEM((LANES, SEQ), F32)],
        compiler_params=pltpu.CompilerParams(vmem_limit_bytes=48 * 2**20),
        cost_estimate=pl.CostEstimate(
            flops=4 * count * SEQ * width,
            bytes_accessed=8 * count * width,
            transcendentals=count * SEQ * width // HD,
        ),
        name="attend",
    )(q, k, v)


def attend_back_kernel(
    side_ref, q_ref, k_ref, v_ref, do_ref, lse_ref, out_ref, sums_ref, dq_t, dk_acc, dv_acc
):
    seq_len = q_ref.shape[0]
    k = k_ref[...]
    v = v_ref[...]
    k_t = k.astype(F32).T.astype(BF16)
    dk_acc[...] = jnp.zeros_like(dk_acc)
    dv_acc[...] = jnp.zeros_like(dv_acc)
    for head in range(2):
        q = head_only(q_ref[...], head)
        do = head_only(do_ref[...], head)
        k_head = k_t[head * HD : (head + 1) * HD, :]
        for start in range(0, seq_len, BACKWARD_BLOCK):
            end = start + BACKWARD_BLOCK
            q_part = q[start:end]
            do_part = do[start:end]
            lse = lse_ref[0, 0, head : head + 1, start:end]
            scores = dot_nt(k[start:end], q_part)
            p_diag = jnp.exp(jnp.where(causal_t(scores), scores, -jnp.inf) - lse)
            dp_diag = dot_nt(v[start:end], do_part)
            inner = jnp.sum(p_diag * dp_diag, axis=0, keepdims=True)
            if start:
                p_full = jnp.exp(dot_nt(k[:start], q_part) - lse)
                dp_full = dot_nt(v[:start], do_part)
                inner = inner + jnp.sum(p_full * dp_full, axis=0, keepdims=True)
                ds_full = (p_full * (dp_full - inner)).astype(BF16)
                dv_acc[:start, :] += dot_nn(p_full.astype(BF16), do_part)
                dk_acc[:start, :] += dot_nn(ds_full, q_part)
            ds_diag = (p_diag * (dp_diag - inner)).astype(BF16)
            dv_acc[start:end, :] += dot_nn(p_diag.astype(BF16), do_part)
            dk_acc[start:end, :] += dot_nn(ds_diag, q_part)
            dq = dot_nn(k_head[:, start:end], ds_diag)
            if start:
                dq = dq + dot_nn(k_head[:, :start], ds_full)
            dq_t[head * HD : (head + 1) * HD, start:end] = dq
    dq = (dq_t[...].T * HD**-0.5).astype(BF16)
    dv = dv_acc[...].astype(BF16)
    out_ref[0] = dq
    out_ref[1] = dk_acc[...].astype(BF16)
    out_ref[2] = dv
    sums_ref[0, 0:1, :] = jnp.sum(dq.astype(F32), axis=0, keepdims=True)
    sums_ref[0, 1:2, :] = jnp.sum(dv.astype(F32), axis=0, keepdims=True)


def attend_back(where, q, k, v, d_attn, lse):
    width = q.shape[1]
    pairs = width // LANES // 2
    block = pl.BlockSpec((SEQ, LANES), lambda p, at: (at[0], at[1] * pairs + p))
    return pl.pallas_call(
        attend_back_kernel,
        grid_spec=pltpu.PrefetchScalarGridSpec(
            num_scalar_prefetch=1,
            grid=(pairs,),
            in_specs=[block] * 4
            + [pl.BlockSpec((1, 1, 2, SEQ), lambda p, at: (at[0], at[1] * pairs + p, 0, 0))],
            out_specs=[
                pl.BlockSpec((3, SEQ, LANES), lambda p, at: (0, 0, p)),
                pl.BlockSpec((1, 2, LANES), lambda p, at: (0, 0, p)),
            ],
            scratch_shapes=[
                pltpu.VMEM((LANES, SEQ), F32),
                pltpu.VMEM((SEQ, LANES), F32),
                pltpu.VMEM((SEQ, LANES), F32),
            ],
        ),
        out_shape=[
            jax.ShapeDtypeStruct((3, SEQ, width // 2), BF16),
            jax.ShapeDtypeStruct((1, 2, width // 2), F32),
        ],
        compiler_params=pltpu.CompilerParams(vmem_limit_bytes=48 * 2**20),
        cost_estimate=pl.CostEstimate(
            flops=5 * SEQ * SEQ * width,
            bytes_accessed=7 * SEQ * width,
            transcendentals=SEQ * SEQ * width // HD // 2,
        ),
        name="attend_back",
    )(where, q, k, v, d_attn, lse)


def weight_grad_kernel(h_ref, *refs):
    grads, (first_ref, second_ref, total) = refs[:-3], refs[-3:]
    step = pl.program_id(0)
    per = pl.num_programs(0) // len(grads)

    @pl.when(step == 0)
    def _():
        total[...] = jnp.zeros_like(total)

    for place, ref in enumerate(grads):
        @pl.when(step // per == place)
        def _():
            total[...] += dot_tn(h_ref[...], jnp.concatenate([ref[0], ref[1], ref[2]], axis=1))

    @pl.when(step == pl.num_programs(0) - 1)
    def _():
        cut = first_ref.shape[1]
        first_ref[...] = total[:, :cut].astype(BF16)
        second_ref[...] = total[:, cut:].astype(BF16)


def weight_grad(h, grads):
    count, width = h.shape
    block = 512
    per = SEQ // block
    cut = 640
    cols = 3 * width // 2

    def spec(place):
        return pl.BlockSpec(
            (3, block, width // 2), lambda i: (0, jnp.clip(i - place * per, 0, per - 1), 0)
        )

    return pl.pallas_call(
        weight_grad_kernel,
        grid=(count // block,),
        in_specs=[rows(block, width)] + [spec(place) for place in range(len(grads))],
        out_specs=[whole((width, cut)), whole((width, cols - cut))],
        out_shape=[
            jax.ShapeDtypeStruct((width, cut), BF16),
            jax.ShapeDtypeStruct((width, cols - cut), BF16),
        ],
        scratch_shapes=[pltpu.VMEM((width, cols), F32)],
        compiler_params=pltpu.CompilerParams(vmem_limit_bytes=48 * 2**20),
        cost_estimate=pl.CostEstimate(
            flops=2 * count * width * cols,
            bytes_accessed=2 * count * (width + cols) + 2 * width * cols,
            transcendentals=0,
        ),
        name="weight_grad",
    )(h, *grads)


LATE_ROWS = 432


def late_parts(packed, wd, wuo, side):
    half = packed.shape[-1]

    def lanes(start):
        return pl.ds(start if isinstance(start, int) else pl.multiple_of(start, LANES), half)

    yield packed.at[:, pl.ds(0, 192), :], wd.at[:, :, lanes(side * half)]
    for block in range(5):
        yield packed.at[:, pl.ds(192 + 48 * block, 48), :], wuo.at[:, :, lanes((side * 5 + block) * half)]


def feed_kernel(*args):
    spots, x_ref, a_ref, dy_ref, vec_ref, ub_ref, late_ref = args[:7]
    mixed_ref, dr_ref, da_ref, gvec_ref, gub_ref, keep_ref, send_ref = args[7:14]
    wd, wuo, acc_d, acc_uo, sem = args[14:]
    step = pl.program_id(0)
    width = x_ref.shape[1]
    up_half = wuo.shape[-1] // 2
    out_first = up_half - width // 2

    def flat(values):
        return values.reshape(width, values.shape[-1])

    def out_weight():
        return jnp.concatenate(
            [flat(wuo[:, :, end - width // 2 : end]) for end in (up_half, 2 * up_half)], axis=1
        )

    @pl.when(step == 0)
    def _():
        copies = []
        for side in range(2):
            for part in late_parts(late_ref.at[:, side], wd, wuo, side):
                copies.append(pltpu.make_async_copy(*part, sem.at[len(copies)]))
                copies[-1].start()
        acc_d[...] = jnp.zeros_like(acc_d)
        acc_uo[...] = jnp.zeros_like(acc_uo)
        gvec_ref[...] = jnp.zeros_like(gvec_ref)
        gub_ref[...] = jnp.zeros_like(gub_ref)
        for copy in copies:
            copy.wait()

    attn = a_ref[...]
    dy = dy_ref[...]
    dy_wide = dy.astype(F32)
    resid = x_ref[...].astype(F32) + dot_nn(attn, out_weight()) + vec_ref[4:5, :]
    normed, rstd = normalise(resid)
    gain = vec_ref[5:6, :]
    h2 = (normed * gain + vec_ref[6:7, :]).astype(BF16)

    def chunk(index, carry):
        mixed, dh2 = carry
        cols = pl.ds(pl.multiple_of(index * width, width), width)
        up_cols = pl.ds(pl.multiple_of(index * width + index // 2 * (width // 2), LANES), width)
        up = flat(wuo[:, :, up_cols])
        down = wd[pl.ds(index * 4, 4)].reshape(width, width)
        u = dot_nn(h2, up) + ub_ref[:, cols]
        d_act = dot_nt(dy, down)
        square = u * u
        tanh = jnp.tanh(GELU_SCALE * u * (1.0 + GELU_CUBIC * square))
        half = 0.5 + 0.5 * tanh
        act = (u * half).astype(BF16)
        slope = half + u * (0.5 - 0.5 * tanh * tanh) * (
            GELU_SCALE * (1.0 + 3.0 * GELU_CUBIC * square)
        )
        du = (d_act * slope).astype(BF16)
        gub_ref[:, cols] += jnp.sum(du.astype(F32), axis=0, keepdims=True)
        acc_d[cols, :] += dot_tn(act, dy)
        acc_uo[:, up_cols] += dot_tn(h2, du)
        return (mixed + dot_nn(act, down), dh2 + dot_nt(du, up))

    mixed, dh2 = lax.fori_loop(
        0, wd.shape[0] // 4, chunk, (resid + vec_ref[7:8, :], jnp.zeros_like(resid))
    )
    mixed_ref[...] = mixed.astype(BF16)
    g = dh2 * gain
    dr = dy_wide + rstd * (
        g
        - jnp.mean(g, axis=-1, keepdims=True)
        - normed * jnp.mean(g * normed, axis=-1, keepdims=True)
    )
    dr_ref[...] = dr
    da = dr.astype(BF16)
    da_ref[...] = dot_nt(da, out_weight()).astype(BF16)
    g_out = dot_tn(attn, da)
    acc_uo[:, out_first:up_half] += g_out[:, : width // 2]
    acc_uo[:, up_half + out_first :] += g_out[:, width // 2 :]
    gvec_ref[0:1, :] += jnp.sum(da.astype(F32), axis=0, keepdims=True)
    gvec_ref[1:2, :] += jnp.sum(dh2 * normed, axis=0, keepdims=True)
    gvec_ref[2:3, :] += jnp.sum(dh2, axis=0, keepdims=True)
    gvec_ref[3:4, :] += jnp.sum(dy_wide, axis=0, keepdims=True)

    @pl.when(step == pl.num_programs(0) - 1)
    def _():
        core = spots[2]
        copies = []
        for side, out in ((1 - core, send_ref), (core, keep_ref)):
            for there, here in late_parts(out, wd, wuo, side):
                copies.append(pltpu.make_async_copy(here, there, sem.at[len(copies)]))
        wd[...] = acc_d[...].astype(BF16).reshape(wd.shape)
        copies[0].start()
        copies[6].start()
        wuo[...] = acc_uo[...].astype(BF16).reshape(wuo.shape)
        for copy in copies[1:6] + copies[7:]:
            copy.start()
        for copy in copies:
            copy.wait()


def feed(spots, tokens, attn, cotangent, vecs, up_bias, late):
    count, width = tokens.shape
    fan = up_bias.shape[1]
    block = 512
    down, up = (16, 192, width), (16, 48, width + fan)
    half = (16, LATE_ROWS, width // 2)
    size = 2 * width * fan + width * width
    return pl.pallas_call(
        feed_kernel,
        grid=(count // block,),
        in_specs=[SMEM_SPEC] + [rows(block, width)] * 3 + [whole(vecs.shape), whole(up_bias.shape), ANY_SPEC],
        out_specs=[rows(block, width)] * 3 + [whole((4, width)), whole(up_bias.shape)] + [ANY_SPEC] * 2,
        out_shape=[
            jax.ShapeDtypeStruct((count, width), BF16),
            jax.ShapeDtypeStruct((count, width), F32),
            jax.ShapeDtypeStruct((count, width), BF16),
            jax.ShapeDtypeStruct((4, width), F32),
            jax.ShapeDtypeStruct(up_bias.shape, F32),
        ] + [jax.ShapeDtypeStruct(half, BF16)] * 2,
        scratch_shapes=[
            pltpu.VMEM(down, BF16),
            pltpu.VMEM(up, BF16),
            pltpu.VMEM((fan, width), F32),
            pltpu.VMEM((width, width + fan), F32),
            pltpu.SemaphoreType.DMA((12,)),
        ],
        compiler_params=pltpu.CompilerParams(vmem_limit_bytes=60 * 2**20),
        cost_estimate=pl.CostEstimate(
            flops=6 * count * size,
            bytes_accessed=14 * count * width + 4 * size,
            transcendentals=count * fan,
        ),
        name="feed",
    )(spots, tokens, attn, cotangent, vecs, up_bias, late)


def input_grad_kernel(*args):
    spots, x_ref, dr_ref, keep_ref, send_ref, vec_ref = args[:6]
    refs, (ig_ref, sums_ref, w, sem) = args[6:14], args[-4:]

    @pl.when(pl.program_id(0) == 0)
    def _():
        copies = load_parts(spots, early_parts(refs), w, sem, swap=True)
        for copy in copies:
            copy.start()
        sums_ref[...] = jnp.zeros_like(sums_ref)
        for copy in copies:
            copy.wait()

    width = x_ref.shape[1]
    half = width // 2
    normed, rstd = normalise(x_ref[...].astype(F32))
    dh = jnp.zeros(x_ref.shape, F32)
    for side, ref in enumerate((keep_ref, send_ref)):
        grads = jnp.concatenate([ref[0], ref[1], ref[2]], axis=1)
        dh = dh + dot_nt(
            grads, w[:, :, :, :, side * 3 * half : (side + 1) * 3 * half].reshape(width, 3 * half)
        )
    g = dh * vec_ref[0:1, :]
    ig_ref[...] = dr_ref[...] + rstd * (
        g
        - jnp.mean(g, axis=-1, keepdims=True)
        - normed * jnp.mean(g * normed, axis=-1, keepdims=True)
    )
    sums_ref[0:1, :] += jnp.sum(dh * normed, axis=0, keepdims=True)
    sums_ref[1:2, :] += jnp.sum(dh, axis=0, keepdims=True)


def input_gradient(spots, tokens, dr, keep, send, vecs, raw, seq, filled=None):
    count, width = tokens.shape
    block = 512
    steps = SEQ // block
    part = pl.BlockSpec((block, width), lambda i: (seq * steps + i, 0))
    third = pl.BlockSpec((3, block, width // 2), lambda i: (0, i, 0))
    extra = [] if filled is None else [filled]
    return pl.pallas_call(
        input_grad_kernel,
        grid=(steps,),
        in_specs=[SMEM_SPEC, part, part, third, third, whole(vecs.shape)] + [ANY_SPEC] * (8 + len(extra)),
        out_specs=[part, whole((2, width))],
        out_shape=[
            jax.ShapeDtypeStruct((count, width), F32),
            jax.ShapeDtypeStruct((2, width), F32),
        ],
        input_output_aliases={14: 0} if extra else {},
        scratch_shapes=[pltpu.VMEM(GRID + (48, 3 * width), BF16), pltpu.SemaphoreType.DMA((8,))],
        compiler_params=pltpu.CompilerParams(vmem_limit_bytes=48 * 2**20),
        cost_estimate=pl.CostEstimate(
            flops=6 * SEQ * width * width,
            bytes_accessed=16 * SEQ * width + 6 * width * width,
            transcendentals=0,
        ),
        name="input_gradient",
    )(spots, tokens, dr, keep, send, vecs, *raw, *extra)


def take(values, index, axis):
    return lax.dynamic_index_in_dim(values, index, axis, keepdims=False)


def wide(values):
    return values.astype(F32)


class Chips:
    def __init__(self):
        me = lax.axis_index("dp")
        self.core = me % 2
        self.strides = (8, 4, 2)
        self.spots = tuple((me // stride) % size for stride, size in zip(self.strides, GRID))

    def pair(self, values):
        return lax.ppermute(values, "dp", [(i, i ^ 1) for i in range(32)])

    def swap(self, values, axis):
        stride = self.strides[axis]
        return lax.ppermute(values, "dp", [(i, i ^ stride) for i in range(32)])

    def turn(self, values, step):
        size, stride = GRID[0], self.strides[0]
        return lax.ppermute(values, "dp", [(i, (i + step * stride) % (size * stride)) for i in range(32)])

    def both(self, spot, own, other, axis):
        return jnp.where(spot == 0, jnp.stack([own, other], axis), jnp.stack([other, own], axis))

    def gather_z(self, own):
        size, spot = GRID[0], self.spots[0]
        seen = [own] + [self.turn(own, step) for step in range(1, size)]
        slots = [lax.select_n(spot, *[seen[(q - p) % size] for q in range(size)]) for p in range(size)]
        return jnp.stack(slots)

    def gather(self, units, last):
        first = 3 - last
        units = self.both(self.spots[first], units, self.swap(units, first), 1)
        other = self.swap(units, last)
        return [units, other, self.pair(units), self.pair(other)]

    def away(self, terms, axis, at, wire):
        return sum(wide(take(term, 1 - self.spots[axis], at)) for term in terms).astype(wire)

    def fold(self, terms, axis, at, wire, away=None):
        away = self.away(terms, axis, at, wire) if away is None else away
        return sum(wide(take(term, self.spots[axis], at)) for term in terms) + wide(self.swap(away, axis))

    def fold_z(self, values, wire):
        size, spot = GRID[0], self.spots[0]
        total = wide(take(values, spot, 0))
        for step in range(1, size):
            away = take(values, (spot + step) % size, 0).astype(wire)
            total = total + wide(self.turn(away, step))
        return total

    def reduce(self, terms, first, wire, away=None):
        if first == 2:
            total = self.fold_z(self.fold(terms, 2, 2, wire, away), wire)
            return self.fold([total], 1, 0, wire)
        total = self.fold(terms, 1, 1, wire, away)
        total = self.fold([total], 2, 1, wire)
        return self.fold_z(total, wire)

    def finish(self, unit):
        share = unit.shape[0] // 2
        mine = lax.dynamic_slice_in_dim(unit, self.core * share, share, 0)
        other = self.pair(lax.dynamic_slice_in_dim(unit, (1 - self.core) * share, share, 0))
        return [jnp.where(self.core == 0, mine, other), jnp.where(self.core == 0, other, mine)]


def halves(parts):
    return [
        jnp.concatenate([part[:, side * part.shape[1] // 2 : (side + 1) * part.shape[1] // 2] for part in parts], axis=1)
        for side in range(2)
    ]


def join(sides, first, last):
    return jnp.concatenate([side[:, first:last] for side in sides], axis=1)


def pack_late(down, up):
    return jnp.concatenate([down] + jnp.split(up, 5, axis=-1), axis=-2)


def unpack_late(packed):
    down, *up = jnp.split(packed, [192, 240, 288, 336, 384], axis=-2)
    return down, jnp.concatenate(up, axis=-1)


def gather_all(chips, shards, small):
    if chips is None:
        early, up, down = (
            jnp.concatenate(halves([lax.all_gather(s, "dp", axis=0, tiled=True) for s in part]), axis=1)
            for part in shards
        )
        small = lax.all_gather(small, "dp", axis=0)

        def parts(axis, first, last):
            unit = early.reshape(GRID + (48, -1))
            cols = unit.shape[-1] // 2
            return [
                take(unit, place, axis)[..., side * cols + first : side * cols + last]
                for side in range(2) for place in range(2)
            ]

        late = jnp.stack(
            [
                pack_late(*(w.reshape(16, -1, 2, w.shape[1] // 2)[:, :, side] for w in (down, up)))
                for side in range(2)
            ],
            axis=1,
        )
        return parts(2, 0, 640) + parts(1, 640, 1152), late, small
    units = []
    for part in shards:
        sides = halves(part)
        mine = jnp.where(chips.core == 0, sides[0], sides[1])
        other = chips.pair(jnp.where(chips.core == 0, sides[1], sides[0]))
        units.append(
            jnp.where(chips.core == 0, jnp.concatenate([mine, other]), jnp.concatenate([other, mine]))
        )
    early_unit, up_unit, down_unit = units
    late = lax.all_gather(pack_late(down_unit, up_unit), "dp", axis=0)
    late = late.reshape(16, 2, LATE_ROWS, -1)
    units = chips.gather_z(jnp.concatenate([early_unit, jnp.pad(small, ((0, 0), (640, 0)))]))
    early = chips.gather(units[:, :48, :640], 2) + chips.gather(units[..., 640:], 1)
    seen = [part[:, :, 48:] for part in early[4:]]
    small = chips.both(
        chips.core,
        chips.both(chips.spots[1], seen[0], seen[1], 1),
        chips.both(chips.spots[1], seen[2], seen[3], 1),
        3,
    )
    return early, late, small.reshape((32,) + small.shape[4:])


def tie(*values):
    return lax.optimization_barrier(values)


def reduce_small(chips, sums):
    if chips is None:
        return lax.psum_scatter(sums, "dp", scatter_dimension=0)
    sums = sums.reshape(GRID + (2, -1))
    other = chips.pair(take(sums, 1 - chips.core, 3))
    return chips.reduce([take(sums, chips.core, 3) + other], 2, F32)


def body(
    tokens, norm_gain, norm_shift, query_weight, query_bias, key_weight, value_weight, value_bias,
    output_weight, output_bias, second_gain, second_shift, up_weight, up_bias, down_weight,
    down_bias, cotangent,
):
    width = tokens.shape[1]
    share = query_weight.shape[0]
    devices = width // share
    fan = up_weight.shape[1]
    half = width // 2
    chips = Chips() if devices == 32 else None
    core = jnp.int32(0) if chips is None else chips.core
    spots = jnp.stack([core, core, core] if chips is None else [chips.spots[1], chips.spots[2], core])

    small = (
        norm_gain, norm_shift, query_bias, value_bias, output_bias, second_gain, second_shift, down_bias, up_bias
    )
    small = sum(
        jnp.pad(values[None], ((row, 15 - row), (0, 512 - values.shape[0]))) for row, values in enumerate(small)
    )
    shards = ([query_weight, key_weight, value_weight], [up_weight, output_weight], [down_weight])
    early, late, small = gather_all(chips, shards, small)
    vecs = wide(
        small[:, :8, :share].transpose(1, 0, 2).reshape(8, width)
    )
    up_bias_all = wide(small[:, 8, : fan // devices].reshape(1, fan))

    h, q, k, v = project(spots, tokens, vecs, early)
    attn, lse = attend(q, k, v)
    mixed, dr, d_attn, vec_sums, up_bias_sum, late_keep, late_send = feed(
        spots, tokens, attn, cotangent, vecs, up_bias_all, late
    )

    seqs = tokens.shape[0] // SEQ

    def back(side, seq, operand):
        where = jnp.stack([jnp.int32(seq), side])
        return attend_back(where, operand, k, v, d_attn, lse)

    def grid(values):
        return values.reshape(GRID + (48, values.shape[-1]))

    if chips is None:
        sends = [back(1 - core, seq, q) for seq in range(seqs)]
        keeps = [back(core, seq, q) for seq in range(seqs)]
        early_send, early_keep = (
            jnp.concatenate(weight_grad(h, [part[0] for part in parts]), axis=1) for parts in (sends, keeps)
        )
        late = [unpack_late(side) for side in (late_keep, late_send)]
        g_down, g_up, g_early = (
            jnp.split(
                wide(
                    lax.psum_scatter(
                        jnp.concatenate([side.reshape(-1, side.shape[-1]) for side in sides], axis=1),
                        "dp", scatter_dimension=0, tiled=True,
                    )
                ),
                2, axis=1,
            )
            for sides in (
                [side[0] for side in late], [side[1] for side in late], [early_keep, early_send]
            )
        )
        input_grad, norm_sums = None, 0.0
        for seq in range(seqs):
            input_grad, more = input_gradient(
                spots, tokens, dr, keeps[seq][0], sends[seq][0], vecs, early, seq, input_grad
            )
            norm_sums = norm_sums + more
    else:
        sends = [back(1 - core, 0, q)]
        late_total = (wide(late_keep) + wide(chips.pair(late_send))).astype(BF16)
        late_total, q = tie(late_total, q)
        late_total = lax.psum_scatter(
            late_total, "dp", scatter_dimension=0, axis_index_groups=[list(range(c, 32, 2)) for c in range(2)]
        )
        sends += [back(1 - core, seq, q) for seq in range(1, seqs)]
        early_send = weight_grad(h, [part[0] for part in sends])
        *early_send, q = tie(*early_send, q)
        early_other = [chips.pair(part) for part in early_send]
        keeps = [back(core, seq, q) for seq in range(seqs)]
        early_keep = weight_grad(h, [part[0] for part in keeps])
        terms = [[grid(own), grid(other)] for own, other in zip(early_keep, early_other)]
        away = [chips.away(terms[0], 2, 2, BF16), chips.away(terms[1], 1, 1, BF16)]
        *away, first = tie(*away, keeps[0][0])
        input_grad, norm_sums = input_gradient(spots, tokens, dr, first, sends[0][0], vecs, early, 0)
        totals = [chips.fold(terms[0], 2, 2, BF16, away[0]), chips.fold(terms[1], 1, 1, BF16, away[1])]
        *totals, last = tie(*totals, keeps[-1][0])
        for seq in range(1, seqs):
            input_grad, more = input_gradient(
                spots, tokens, dr, last if seq == seqs - 1 else keeps[seq][0], sends[seq][0], vecs, early, seq, input_grad
            )
            norm_sums = norm_sums + more
        first, second = chips.fold([totals[0]], 1, 1, BF16), chips.fold([totals[1]], 2, 1, BF16)
        g_early = chips.finish(chips.fold_z(jnp.concatenate([first, second], axis=2), BF16))
        down, up = unpack_late(wide(late_total))
        g_down, g_up = chips.finish(down), chips.finish(up)
    sums_keep, sums_send = (sum(part[1][0] for part in parts) for parts in (keeps, sends))
    bias_sums = jnp.where(
        core == 0,
        jnp.concatenate([sums_keep, sums_send], axis=1),
        jnp.concatenate([sums_send, sums_keep], axis=1),
    )
    sums = jnp.concatenate([norm_sums, bias_sums, vec_sums])
    sums = sums.reshape(8, devices, share).transpose(1, 0, 2).reshape(devices, 8 * share)
    sums = jnp.concatenate([sums, up_bias_sum.reshape(devices, fan * share // width)], axis=1)
    sums = reduce_small(chips, sums)
    vec_grads = [sums[place * share : (place + 1) * share] for place in range(8)]
    g_wq, g_wk, g_wv = (join(g_early, place * half, (place + 1) * half) for place in range(3))
    return (
        mixed, input_grad,
        vec_grads[0], vec_grads[1], g_wq, vec_grads[2], g_wk, g_wv, vec_grads[3],
        join(g_up, fan // 2, (fan + width) // 2), vec_grads[4], vec_grads[5], vec_grads[6],
        join(g_up, 0, fan // 2), sums[8 * share :], join(g_down, 0, half), vec_grads[7],
    )


def solution(mesh):
    row, vec = P("dp", None), P("dp")
    params = (vec, vec, row, vec, row, row, vec, row, vec, vec, vec, row, vec, row, vec)
    return jax.shard_map(
        body,
        mesh=mesh,
        in_specs=(row, *params, row),
        out_specs=(row, row, *params),
        check_vma=False,
    )
```
